32 devices in a mesh: seq: 8 (over y, x, core), head: 4 (over z).
Axes of the slice: x: 2, y: 2, z: 4, core: 2. Of those that a mesh axis runs over, the one named last changes fastest.
Arguments:
- qkv: bfloat16 [4096, 4096], P(('seq', 'head')), may hold values from -24 to 24
- residual: bfloat16 [4096, 2048], P(('seq', 'head')), may hold values from -1.5 to 1.5
- dest_row: int32 [4096], P(('seq', 'head')), may hold values from 0 to 4095, as said below
- source_row: int32 [4096], P(('seq', 'head')), may hold values from 0 to 4095, as said below
- doc_start: int32 [4096], P('seq'), may hold values from 0 to 511, as said below
- out_weight: bfloat16 [3072, 2048], P('head'), may hold values from -0.109375 to 0.109375
- norm_gain: float32 [2048], replicated, may hold values from 0.5 to 1.5
Outputs:
- new_residual: bfloat16 [4096, 2048], P(('seq', 'head'))
- normed: bfloat16 [4096, 2048], P(('seq', 'head'))
The draws below stay inside these ranges and needn't reach their ends.
Inputs may be any that keep to these rules, and one draw needn't show every extreme that they name: `dest_row`: A permutation of all rows. Row (s * 4 + h) * 128 + r goes to a place (g * 4 + h) * 128 + p with the same h. Of the 128 rows of one device, at most 24 go to one group g, every device sends exactly 24 rows to at least one group, and every device receives exactly 24 rows from at least one sender. `source_row`: the inverse permutation of dest_row. Documents are runs of consecutive rows inside one group: doc_start of a row is at most its own group-local index and equals that of the previous row unless the row begins a document; the first row of a group begins a document.
All inputs are finite; a program needn't handle non-finite values.
Results may differ from the reference program's by a relative error of at most 0.014.
Values may be sent and summed in bfloat16 or wider, within the bound.
A program may use at most 64 MiB of HBM per device.

```python
import jax
import jax.numpy as jnp
from jax import lax

D = 2048
QH = 24
KVH = 4
HD = 128
TOK_DEV = 128
CAP = 24
GROUP = 512
TOKENS = 4096
QKV = 4096
N_SEQ = 8
N_HEAD = 4


def regroup_tables(key):
    base = jax.random.fold_in(key, 11)
    senders = N_SEQ
    places = N_SEQ * TOK_DEV

    def column(colkey, headidx):
        keys = jax.random.split(colkey, 5)
        chosen = jax.random.permutation(keys[0], (senders - 1) * CAP)[:TOK_DEV - CAP]
        counts = jnp.zeros((senders,), jnp.int32).at[chosen // CAP + 1].add(1)
        counts = counts + jnp.where(jnp.arange(senders) == 0, CAP, 0).astype(jnp.int32)
        bounds = jnp.cumsum(counts)
        binof = jnp.sum((jnp.arange(TOK_DEV)[:, None] >= bounds[None, :]).astype(jnp.int32), axis=1)
        sigma = jax.random.permutation(keys[1], senders)
        tau = jax.random.permutation(keys[2], senders)
        rowperm = jax.vmap(lambda k: jax.random.permutation(k, TOK_DEV))(jax.random.split(keys[3], senders))
        bins = binof[rowperm]
        target = sigma[(tau[:, None] + bins) % senders]
        flat = target.reshape(-1)
        noise = jax.random.permutation(keys[4], places)
        order = jnp.argsort(flat * places + noise, stable=True)
        ranks = jnp.arange(places, dtype=jnp.int32)
        dest_sorted = (ranks // TOK_DEV * N_HEAD + headidx) * TOK_DEV + ranks % TOK_DEV
        dest_flat = jnp.zeros((places,), jnp.int32).at[order].set(dest_sorted.astype(jnp.int32))
        return dest_flat.reshape(senders, TOK_DEV)
    columns = jax.vmap(column)(jax.random.split(base, N_HEAD), jnp.arange(N_HEAD, dtype=jnp.int32))
    dest = jnp.transpose(columns, (1, 0, 2)).reshape(-1).astype(jnp.int32)
    source = jnp.zeros((TOKENS,), jnp.int32).at[dest].set(jnp.arange(TOKENS, dtype=jnp.int32))
    return (dest, source)


def draw_dest_row(key, part):
    return regroup_tables(key)[0]


def draw_source_row(key, part):
    return regroup_tables(key)[1]


def draw_doc_start(key, part):
    first, second = jax.random.split(jax.random.fold_in(key, 7))
    levels = max(1, (GROUP // 8).bit_length())
    exponent = jax.random.randint(first, (N_SEQ, 1), 0, levels)
    spacing = jnp.left_shift(jnp.int32(8), exponent.astype(jnp.int32))
    raw = jax.random.randint(second, (N_SEQ, GROUP), 0, 1 << 20)
    places = jnp.arange(GROUP, dtype=jnp.int32)
    begins = (raw % spacing == 0) | (places[None, :] == 0)
    marker = jnp.where(begins, places[None, :], 0).astype(jnp.int32)
    return lax.cummax(marker, axis=1).reshape(-1).astype(jnp.int32)


def draw_qkv(key, part):
    keys = jax.random.split(jax.random.fold_in(key, 3), 1)
    whole = jnp.clip(jax.random.normal(keys[0], (TOKENS, QKV), jnp.float32), -6.0, 6.0)
    return whole.astype(jnp.bfloat16)


def block_scale(key, shape, cuts, low, high):
    gain, own = 1.0, jax.random.fold_in(key, 6)
    for axis_at, shards_of in cuts:
        heights = jnp.exp(jax.random.uniform(jax.random.fold_in(own, axis_at), (shards_of,), jnp.float32, low / len(cuts), high / len(cuts)))
        gain = gain * jnp.repeat(heights, shape[axis_at] // shards_of).reshape([-1 if axis == axis_at else 1 for axis in range(len(shape))])
    return gain


def scatter_about(key, shape, deviation, limit, cuts=(), kind=jnp.bfloat16):
    level = block_scale(key, shape, cuts, -0.22, 0.18) if cuts else 1.0
    values = jax.random.normal(key, shape, jnp.float32) * deviation * level
    return jnp.minimum(jnp.maximum(values, -limit), limit).astype(kind)


def setup_inputs(seed: int = 0) -> dict:
    streams_of = jax.random.split(jax.random.key(seed), 8)
    return {
        "qkv": draw_qkv(jax.random.fold_in(streams_of[7], 71), 0),
        "residual": scatter_about(streams_of[1], (TOKENS, D), 0.25, 1.5, ((0, 32),)),
        "dest_row": draw_dest_row(jax.random.fold_in(streams_of[7], 71), 0),
        "source_row": draw_source_row(jax.random.fold_in(streams_of[7], 71), 0),
        "doc_start": draw_doc_start(jax.random.fold_in(streams_of[7], 71), 0),
        "out_weight": scatter_about(streams_of[5], (QH * HD, D), (QH * HD) ** -0.5, 0.109375, ((0, 4),)),
        "norm_gain": jnp.clip(1.0 + 0.1 * jax.random.normal(streams_of[6], (D,), jnp.float32), 0.5, 1.5),
    }


def reference(qkv, residual, dest_row, source_row, doc_start, out_weight, norm_gain):
    group_rows = TOK_DEV * N_HEAD
    shared = QH // KVH
    qwidth = QH * HD
    kwidth = KVH * HD
    ordered = qkv[source_row]
    blocks = ordered.reshape(N_SEQ, group_rows, qwidth + 2 * kwidth)
    starts = doc_start.reshape(N_SEQ, group_rows)

    def attend(item):
        rows, first = item
        query = rows[:, :qwidth].reshape(group_rows, QH, HD).astype(jnp.float32)
        keys = rows[:, qwidth:qwidth + kwidth].reshape(group_rows, KVH, HD).astype(jnp.float32)
        values = rows[:, qwidth + kwidth:].reshape(group_rows, KVH, HD).astype(jnp.float32)
        keys = jnp.repeat(keys, shared, axis=1)
        values = jnp.repeat(values, shared, axis=1)
        scores = jnp.einsum('qhd,khd->hqk', query, keys) * HD ** (-0.5)
        places = jnp.arange(group_rows, dtype=jnp.int32)
        visible = (places[None, :] <= places[:, None]) & (places[None, :] >= first[:, None])
        scores = jnp.where(visible[None], scores, -1e+30)
        top = lax.optimization_barrier(jnp.max(scores, axis=-1, keepdims=True))
        weights = jnp.exp(scores - top)
        total = lax.optimization_barrier(jnp.sum(weights, axis=-1, keepdims=True))
        probs = lax.optimization_barrier(weights.astype(jnp.bfloat16)).astype(jnp.float32)
        numer = jnp.einsum('hqk,khd->qhd', probs, values)
        result = numer / jnp.transpose(total, (1, 0, 2))
        return result.astype(jnp.bfloat16).reshape(group_rows, qwidth)
    attn = lax.map(attend, (blocks, starts)).reshape(TOKENS, qwidth)
    share = QH // N_HEAD * HD
    summed = jnp.zeros((TOKENS, D), jnp.float32)
    for block in range(N_HEAD):
        part = jnp.dot(attn[:, block * share:(block + 1) * share], out_weight[block * share:(block + 1) * share], preferred_element_type=jnp.float32)
        summed = summed + lax.optimization_barrier(part.astype(jnp.bfloat16)).astype(jnp.float32)
    proj = summed.astype(jnp.bfloat16)
    arrived = proj[dest_row]
    new_residual = (residual.astype(jnp.float32) + arrived.astype(jnp.float32)).astype(jnp.bfloat16)
    stream = lax.optimization_barrier(new_residual).astype(jnp.float32)
    scale = lax.rsqrt(lax.optimization_barrier(jnp.mean(stream * stream, axis=-1, keepdims=True)) + 1e-06)
    normed = (stream * scale * norm_gain).astype(jnp.bfloat16)
    return (new_residual, normed)
```

```python
import functools

import jax
import jax.numpy as jnp
import numpy as np
from jax import lax
from jax.experimental import pallas as pl
from jax.experimental.pallas import tpu as pltpu
from jax.sharding import PartitionSpec as P

QH = 24
KVH = 4
HD = 128
MESH = pl.DeviceIdType.MESH


def one_hot_slots(member, ranks, n_seq, cap):
    rows = member.shape[1]
    rank = jnp.where(member, ranks.astype(jnp.int32), -4 * cap)
    place = lax.broadcasted_iota(jnp.int32, (n_seq, 2 * cap, rows), 1)
    low = (rank[:, None, :] == place).astype(jnp.float32).reshape(n_seq * 2 * cap, rows)
    high = (rank[:, None, :] + cap == place).astype(jnp.float32).reshape(n_seq * 2 * cap, rows)
    return low, high


def kernel(
    n_seq, n_head, cap, jobs,
    qkv, residual, dest, source, starts, weight, gain,
    out_res, out_norm,
    w_vmem, p_one, pt_one, r_one, rt_one, x_send, x_recv, z_send, z_recv, attn,
    s_send, s_recv, acc, b_send, b_recv,
    w_sem, xs_sem, xr_sem, zs_sem, zr_sem, ss_sem, sr_sem, bs_sem, br_sem,
):
    f32, bf16 = jnp.float32, jnp.bfloat16
    seq, head = lax.axis_index("seq"), lax.axis_index("head")
    tok = qkv.shape[0]
    group = tok * n_head
    heads_here = weight.shape[0] // HD
    shared = QH // KVH
    width = x_send.shape[3] * 2
    half = width // 2
    cols = weight.shape[1] // jobs
    slots = n_seq * 2 * cap

    def dot(a, b):
        return jnp.dot(a, b, preferred_element_type=f32)

    def wait_bytes(ref, sem):
        pltpu.make_async_copy(ref, ref, sem).wait()

    load_w = pltpu.make_async_copy(weight, w_vmem, w_sem)
    load_w.start()

    barrier = pltpu.get_barrier_semaphore()

    @pl.loop(1, n_seq)
    def _(i):
        pl.semaphore_signal(barrier, inc=1, device_id=((seq + i) % n_seq, head), device_id_type=MESH)

    @pl.loop(1, n_head)
    def _(i):
        pl.semaphore_signal(barrier, inc=1, device_id=(seq, (head + i) % n_head), device_id_type=MESH)

    bounds = lax.broadcasted_iota(jnp.int32, (n_seq, tok), 0) * group
    goes = (dest[...] >= bounds) & (dest[...] < bounds + group)
    comes = (source[...] >= bounds) & (source[...] < bounds + group)
    earlier = lax.broadcasted_iota(jnp.int32, (tok, tok), 0) < lax.broadcasted_iota(jnp.int32, (tok, tok), 1)
    low, high = one_hot_slots(goes, dot(goes.astype(f32).astype(bf16), earlier.astype(f32).astype(bf16)), n_seq, cap)
    p_one[0], p_one[1] = low.astype(bf16), high.astype(bf16)

    pl.semaphore_wait(barrier, n_seq + n_head - 2)

    shifts = sorted(range(n_head), key=lambda s: (s == 0, abs(s - n_head / 2), -s))
    for c, shift in enumerate(shifts):
        to = (head + shift) % n_head
        kv = (to * heads_here) // shared
        query = qkv[:, pl.ds(pl.multiple_of(to * heads_here * HD, HD), heads_here * HD)]
        key = qkv[:, pl.ds(pl.multiple_of(QH * HD + kv * HD, HD), HD)]
        value = qkv[:, pl.ds(pl.multiple_of((QH + KVH) * HD + kv * HD, HD), HD)]
        x = jnp.concatenate([query, key, value], axis=1)
        placed = (dot(p_one[0], x[:, :half]) + dot(p_one[1], x[:, half:])).astype(bf16)
        x_send[c] = placed.reshape(n_seq, 2 * cap, half)
        x_recv[c, pl.ds(seq, 1)] = x_send[c, pl.ds(seq, 1)]

        @pl.loop(1, n_seq)
        def _(i):
            peer = (seq + i) % n_seq
            pltpu.make_async_remote_copy(
                src_ref=x_send.at[c, peer], dst_ref=x_recv.at[c, seq],
                send_sem=xs_sem.at[c], recv_sem=xr_sem.at[c],
                device_id=(peer, head), device_id_type=MESH,
            ).start()

        if c == 0:
            pt_one[0], pt_one[1] = low.T.astype(bf16), high.T.astype(bf16)
            across = jnp.broadcast_to(source[...].astype(f32), (tok, tok))
            before = (across.T < across).astype(f32).astype(bf16)
            rlow, rhigh = one_hot_slots(comes, dot(comes.astype(f32).astype(bf16), before), n_seq, cap)
            r_one[0], r_one[1] = rlow.astype(bf16), rhigh.astype(bf16)
            rt_one[0], rt_one[1] = rlow.T.astype(bf16), rhigh.T.astype(bf16)

    for c, shift in enumerate(shifts):
        to = (head + shift) % n_head
        wait_bytes(x_recv.at[c, pl.ds(0, n_seq - 1)], xr_sem.at[c])
        arrived = x_recv[c].reshape(slots, half)
        rows = jnp.concatenate([dot(rt_one[0], arrived), dot(rt_one[1], arrived)], axis=1).astype(bf16)
        if shift == 0:
            z_recv[pl.ds(head, 1)] = rows[None]
        else:
            z_send[c] = rows
            pltpu.make_async_remote_copy(
                src_ref=z_send.at[c], dst_ref=z_recv.at[head],
                send_sem=zs_sem.at[c], recv_sem=zr_sem.at[head],
                device_id=(seq, to), device_id_type=MESH,
            ).start()

    @pl.loop(1, n_head)
    def _(i):
        other = (head + i) % n_head
        wait_bytes(z_recv.at[other], zr_sem.at[other])

    factor = HD ** (-0.5) * float(np.log2(np.e))
    kcol = heads_here * HD
    for i in range(n_head):
        span = (i + 1) * tok
        keys = z_recv[: i + 1, :, kcol : kcol + HD].reshape(span, HD)
        values = z_recv[: i + 1, :, kcol + HD : kcol + 2 * HD].reshape(span, HD)
        first = jnp.broadcast_to(starts[:, i * tok : (i + 1) * tok].astype(f32), (tok, tok)).T[:, :1]
        kplace = lax.broadcasted_iota(jnp.int32, (tok, span), 1)
        qplace = lax.broadcasted_iota(jnp.int32, (tok, span), 0) + i * tok
        visible = (kplace <= qplace) & (kplace >= first.astype(jnp.int32))
        for a in range(heads_here):
            scores = lax.dot_general(
                z_recv[i, :, a * HD : (a + 1) * HD], keys, (((1,), (1,)), ((), ())), preferred_element_type=f32
            )
            scores = jnp.where(visible, scores, -1e30)
            top = jnp.max(scores, axis=-1, keepdims=True)
            weights = jnp.exp2((scores - top) * factor)
            total = jnp.sum(weights, axis=-1, keepdims=True)
            attn[i, :, a * HD : (a + 1) * HD] = (dot(weights.astype(bf16), values) / total).astype(bf16)

    load_w.wait()

    def partial(block, j):
        return dot(attn[block], w_vmem[:, pl.ds(pl.multiple_of(j * cols, cols), cols)])

    @pl.loop(0, n_head - 1)
    def _(t):
        above, below = n_head - 1 - t, t

        @pl.loop(0, jobs)
        def _(j):
            @pl.when(above > head)
            def _():
                acc[...] = partial(above, j)

                @pl.when(head > 0)
                def _():
                    wait_bytes(s_recv.at[above + 1, j], sr_sem.at[above + 1, j])
                    acc[...] += s_recv[above + 1, j].astype(f32)

                s_send[above, j] = acc[...].astype(bf16)
                pltpu.make_async_remote_copy(
                    src_ref=s_send.at[above, j], dst_ref=s_recv.at[above + 1, j],
                    send_sem=ss_sem.at[above, j], recv_sem=sr_sem.at[above + 1, j],
                    device_id=(seq, head + 1), device_id_type=MESH,
                ).start()

            @pl.when(below < head)
            def _():
                acc[...] = partial(below, j)

                @pl.when(head < n_head - 1)
                def _():
                    wait_bytes(s_recv.at[below, j], sr_sem.at[below, j])
                    acc[...] += s_recv[below, j].astype(f32)

                s_send[below, j] = acc[...].astype(bf16)
                pltpu.make_async_remote_copy(
                    src_ref=s_send.at[below, j], dst_ref=s_recv.at[below, j],
                    send_sem=ss_sem.at[below, j], recv_sem=sr_sem.at[below, j],
                    device_id=(seq, head - 1), device_id_type=MESH,
                ).start()

    quarter = cols // 2

    @pl.loop(0, jobs)
    def _(j):
        acc[...] = partial(head, j)

        @pl.when(head > 0)
        def _():
            wait_bytes(s_recv.at[head + 1, j], sr_sem.at[head + 1, j])
            acc[...] += s_recv[head + 1, j].astype(f32)

        @pl.when(head < n_head - 1)
        def _():
            wait_bytes(s_recv.at[head, j], sr_sem.at[head, j])
            acc[...] += s_recv[head, j].astype(f32)

        proj = acc[...].astype(bf16)
        back = (dot(r_one[0], proj[:, :quarter]) + dot(r_one[1], proj[:, quarter:])).astype(bf16)
        b_send[j] = back.reshape(n_seq, 2 * cap, quarter)
        b_recv[j, pl.ds(seq, 1)] = b_send[j, pl.ds(seq, 1)]

        @pl.loop(1, n_seq)
        def _(i):
            peer = (seq + i) % n_seq
            pltpu.make_async_remote_copy(
                src_ref=b_send.at[j, peer], dst_ref=b_recv.at[j, seq],
                send_sem=bs_sem.at[j], recv_sem=br_sem.at[j],
                device_id=(peer, head), device_id_type=MESH,
            ).start()

    square = jnp.zeros((tok, 1), f32)
    for j in range(jobs):
        wait_bytes(b_recv.at[j, pl.ds(0, n_seq - 1)], br_sem.at[j])
        arrived = b_recv[j].reshape(slots, quarter)
        mine = jnp.concatenate([dot(pt_one[0], arrived), dot(pt_one[1], arrived)], axis=1)
        here = slice(j * cols, (j + 1) * cols)
        stream = (residual[:, here].astype(f32) + mine).astype(bf16)
        out_res[:, here] = stream
        wide = stream.astype(f32)
        square += jnp.sum(wide * wide, axis=-1, keepdims=True)
    scale = lax.rsqrt(square / (jobs * cols) + 1e-06)
    for j in range(jobs):
        here = slice(j * cols, (j + 1) * cols)
        out_norm[:, here] = (out_res[:, here].astype(f32) * scale * gain[:, here]).astype(bf16)

    for c, shift in enumerate(shifts):
        wait_bytes(x_send.at[c, pl.ds(0, n_seq - 1)], xs_sem.at[c])
        if shift != 0:
            wait_bytes(z_send.at[c], zs_sem.at[c])

    @pl.loop(0, jobs)
    def _(j):
        wait_bytes(b_send.at[j, pl.ds(0, n_seq - 1)], bs_sem.at[j])

        @pl.loop(1, n_head)
        def _(i):
            block = (head + i) % n_head
            wait_bytes(s_send.at[block, j], ss_sem.at[block, j])


def local(qkv, residual, dest_row, source_row, doc_start, out_weight, norm_gain):
    n_seq = lax.axis_size("seq")
    n_head = lax.axis_size("head")
    tok, _ = qkv.shape
    depth, model = out_weight.shape
    cap = -(-max(2, 3 * tok // (2 * n_seq)) // 8) * 8
    jobs = 4
    width = depth + 2 * HD
    cols = model // jobs
    bf16 = jnp.bfloat16
    dma = pltpu.SemaphoreType.DMA
    vmem = pl.BlockSpec(memory_space=pltpu.VMEM)
    return pl.pallas_call(
        functools.partial(kernel, n_seq, n_head, cap, jobs),
        out_shape=(jax.ShapeDtypeStruct(residual.shape, bf16), jax.ShapeDtypeStruct(residual.shape, bf16)),
        in_specs=[vmem, vmem, vmem, vmem, vmem, pl.BlockSpec(memory_space=pl.ANY), vmem],
        out_specs=(vmem, vmem),
        scratch_shapes=[
            pltpu.VMEM((depth, model), bf16),
            pltpu.VMEM((2, n_seq * 2 * cap, tok), bf16),
            pltpu.VMEM((2, tok, n_seq * 2 * cap), bf16),
            pltpu.VMEM((2, n_seq * 2 * cap, tok), bf16),
            pltpu.VMEM((2, tok, n_seq * 2 * cap), bf16),
            pltpu.VMEM((n_head, n_seq, 2 * cap, width // 2), bf16),
            pltpu.VMEM((n_head, n_seq, 2 * cap, width // 2), bf16),
            pltpu.VMEM((n_head, tok, width), bf16),
            pltpu.VMEM((n_head, tok, width), bf16),
            pltpu.VMEM((n_head, tok, depth), bf16),
            pltpu.VMEM((n_head, jobs, tok, cols), bf16),
            pltpu.VMEM((n_head + 1, jobs, tok, cols), bf16),
            pltpu.VMEM((tok, cols), jnp.float32),
            pltpu.VMEM((jobs, n_seq, 2 * cap, cols // 2), bf16),
            pltpu.VMEM((jobs, n_seq, 2 * cap, cols // 2), bf16),
            dma,
            dma((n_head,)),
            dma((n_head,)),
            dma((n_head,)),
            dma((n_head,)),
            dma((n_head, jobs)),
            dma((n_head + 1, jobs)),
            dma((jobs,)),
            dma((jobs,)),
        ],
        compiler_params=pltpu.CompilerParams(
            collective_id=0, has_side_effects=True, vmem_limit_bytes=56 * 1024 * 1024
        ),
        name="layer",
    )(
        qkv,
        residual,
        dest_row.reshape(1, tok),
        source_row.reshape(1, tok),
        doc_start.reshape(1, tok * n_head),
        out_weight,
        norm_gain.reshape(1, model),
    )


def solution(mesh):
    return jax.shard_map(
        local,
        mesh=mesh,
        in_specs=(
            P(("seq", "head"), None),
            P(("seq", "head"), None),
            P(("seq", "head")),
            P(("seq", "head")),
            P("seq"),
            P("head", None),
            P(),
        ),
        out_specs=(P(("seq", "head"), None), P(("seq", "head"), None)),
        check_vma=False,
    )
```

```python
import functools

import jax
import jax.numpy as jnp
import numpy as np
from jax import lax
from jax.experimental import pallas as pl
from jax.experimental.pallas import tpu as pltpu
from jax.sharding import PartitionSpec as P

QH = 24
KVH = 4
HD = 128
MESH = pl.DeviceIdType.MESH


def one_hot_slots(member, ranks, n_seq, cap):
    rows = member.shape[1]
    rank = jnp.where(member, ranks.astype(jnp.int32), -4 * cap)
    place = lax.broadcasted_iota(jnp.int32, (n_seq, 2 * cap, rows), 1)
    low = (rank[:, None, :] == place).astype(jnp.float32).reshape(n_seq * 2 * cap, rows)
    high = (rank[:, None, :] + cap == place).astype(jnp.float32).reshape(n_seq * 2 * cap, rows)
    return low, high


def kernel(
    n_seq, n_head, cap, jobs,
    qkv, dest, source, starts, weight,
    out,
    w_vmem, p_one, pt_one, r_one, rt_one, kx_send, kx_recv, x_send, x_recv, kv_rows, k_send, kv_recv,
    z_send, q_recv, attn, s_send, s_recv, acc, b_send, b_recv,
    w_sem, kxs_sem, kxr_sem, xs_sem, xr_sem, ks_sem, kr_sem, zs_sem, zr_sem, ss_sem, sr_sem, bs_sem, br_sem,
):
    f32, bf16 = jnp.float32, jnp.bfloat16
    seq, head = lax.axis_index("seq"), lax.axis_index("head")
    tok = qkv.shape[0]
    group = tok * n_head
    heads_here = weight.shape[0] // HD
    shared = QH // KVH
    cols = weight.shape[1] // jobs
    slots = n_seq * 2 * cap

    def dot(a, b):
        return jnp.dot(a, b, preferred_element_type=f32)

    def wait_bytes(ref, sem):
        pltpu.make_async_copy(ref, ref, sem).wait()

    load_w = pltpu.make_async_copy(weight, w_vmem, w_sem)
    load_w.start()

    barrier = pltpu.get_barrier_semaphore()

    @pl.loop(1, n_seq)
    def _(i):
        pl.semaphore_signal(barrier, inc=1, device_id=((seq + i) % n_seq, head), device_id_type=MESH)

    @pl.loop(1, n_head)
    def _(i):
        pl.semaphore_signal(barrier, inc=1, device_id=(seq, (head + i) % n_head), device_id_type=MESH)

    bounds = lax.broadcasted_iota(jnp.int32, (n_seq, tok), 0) * group
    goes = (dest[...] >= bounds) & (dest[...] < bounds + group)
    comes = (source[...] >= bounds) & (source[...] < bounds + group)
    earlier = lax.broadcasted_iota(jnp.int32, (tok, tok), 0) < lax.broadcasted_iota(jnp.int32, (tok, tok), 1)
    low, high = one_hot_slots(goes, dot(goes.astype(f32).astype(bf16), earlier.astype(f32).astype(bf16)), n_seq, cap)
    p_one[0], p_one[1] = low.astype(bf16), high.astype(bf16)

    pl.semaphore_wait(barrier, n_seq + n_head - 2)

    def partner(c):
        if n_head == 4:
            mirror = n_head - 1 - head
            return [mirror, (head + 2) % n_head, (mirror + 2) % n_head, head][c]
        return (shifts[c] - head + n_head) % n_head

    def place(x, send, recv, s_sem, r_sem):
        side = x.shape[1] // 2
        placed = (dot(p_one[0], x[:, :side]) + dot(p_one[1], x[:, side:])).astype(bf16)
        send[...] = placed.reshape(n_seq, 2 * cap, side)
        recv[pl.ds(seq, 1)] = send[pl.ds(seq, 1)]

        @pl.loop(1, n_seq)
        def _(i):
            peer = (seq + i) % n_seq
            pltpu.make_async_remote_copy(
                src_ref=send.at[peer], dst_ref=recv.at[seq],
                send_sem=s_sem, recv_sem=r_sem,
                device_id=(peer, head), device_id_type=MESH,
            ).start()

    def gather(recv, r_sem):
        wait_bytes(recv.at[pl.ds(0, n_seq - 1)], r_sem)
        arrived = recv[...].reshape(slots, recv.shape[2])
        return jnp.concatenate([dot(rt_one[0], arrived), dot(rt_one[1], arrived)], axis=1).astype(bf16)

    shifts = [(n_head - 1 + c) % n_head for c in range(n_head)]
    depth = heads_here * HD
    place(qkv[:, QH * HD :], kx_send, kx_recv, kxs_sem, kxr_sem)

    low_t, high_t = low.T, high.T
    pt_one[0], pt_one[1] = low_t.astype(bf16), high_t.astype(bf16)
    across = jnp.broadcast_to(source[...].astype(f32), (tok, tok))
    before = (across.T < across).astype(f32).astype(bf16)
    rlow, rhigh = one_hot_slots(comes, dot(comes.astype(f32).astype(bf16), before), n_seq, cap)
    r_one[0], r_one[1] = rlow.astype(bf16), rhigh.astype(bf16)
    rt_one[0], rt_one[1] = rlow.T.astype(bf16), rhigh.T.astype(bf16)

    for c in range(n_head):
        query = qkv[:, pl.ds(pl.multiple_of(partner(c) * depth, HD), depth)]
        place(query, x_send.at[c], x_recv.at[c], xs_sem.at[c], xr_sem.at[c])

    kv_rows[...] = gather(kx_recv, kxr_sem)

    def kv_of(block):
        kv = (block * heads_here) // shared
        key = kv_rows[:, pl.ds(pl.multiple_of(kv * HD, HD), HD)]
        value = kv_rows[:, pl.ds(pl.multiple_of((KVH + kv) * HD, HD), HD)]
        return jnp.concatenate([key, value], axis=1)

    kv_recv[pl.ds(head, 1)] = kv_of(head)[None]
    for c in range(1, n_head):
        to = (head + c) % n_head
        k_send[c] = kv_of(to)
        pltpu.make_async_remote_copy(
            src_ref=k_send.at[c], dst_ref=kv_recv.at[head],
            send_sem=ks_sem.at[c], recv_sem=kr_sem.at[head],
            device_id=(seq, to), device_id_type=MESH,
        ).start()

    for c in range(n_head):
        rows = gather(x_recv.at[c], xr_sem.at[c])
        to = partner(c)
        z_send[c] = rows

        @pl.when(to == head)
        def _():
            q_recv[pl.ds(head, 1)] = z_send[pl.ds(c, 1)]

        @pl.when(to != head)
        def _():
            pltpu.make_async_remote_copy(
                src_ref=z_send.at[c], dst_ref=q_recv.at[head],
                send_sem=zs_sem.at[c], recv_sem=zr_sem.at[head],
                device_id=(seq, to), device_id_type=MESH,
            ).start()

    @pl.loop(1, n_head)
    def _(i):
        other = (head + i) % n_head
        wait_bytes(kv_recv.at[other], kr_sem.at[other])

    load_w.wait()
    factor = HD ** (-0.5) * float(np.log2(np.e))

    def attend(i):
        span = (i + 1) * tok
        keys = kv_recv[: i + 1, :, :HD].reshape(span, HD)
        values = kv_recv[: i + 1, :, HD:].reshape(span, HD)
        first = jnp.broadcast_to(starts[:, i * tok : (i + 1) * tok].astype(f32), (tok, tok)).T[:, :1]
        kplace = lax.broadcasted_iota(jnp.int32, (tok, span), 1)
        qplace = lax.broadcasted_iota(jnp.int32, (tok, span), 0) + i * tok
        visible = (kplace <= qplace) & (kplace >= first.astype(jnp.int32))
        for a in range(heads_here):
            scores = lax.dot_general(
                q_recv[i, :, a * HD : (a + 1) * HD], keys, (((1,), (1,)), ((), ())), preferred_element_type=f32
            )
            scores = jnp.where(visible, scores, -1e30)
            top = jnp.max(scores, axis=-1, keepdims=True)
            weights = jnp.exp2((scores - top) * factor)
            total = jnp.sum(weights, axis=-1, keepdims=True)
            attn[i, :, a * HD : (a + 1) * HD] = (dot(weights.astype(bf16), values) / total).astype(bf16)

    def partial(block, j):
        return dot(attn[block], w_vmem[:, pl.ds(pl.multiple_of(j * cols, cols), cols)])

    def step(block, j):
        up = block > head
        slot = jnp.where(up, block + 1, block)
        acc[...] = partial(block, j)

        @pl.when((head > 0) & (head < n_head - 1))
        def _():
            wait_bytes(s_recv.at[slot, j], sr_sem.at[slot, j])
            acc[...] += s_recv[slot, j].astype(f32)

        s_send[block, j] = acc[...].astype(bf16)
        pltpu.make_async_remote_copy(
            src_ref=s_send.at[block, j], dst_ref=s_recv.at[slot, j],
            send_sem=ss_sem.at[block, j], recv_sem=sr_sem.at[slot, j],
            device_id=(seq, jnp.where(up, head + 1, head - 1)), device_id_type=MESH,
        ).start()

    end = (head == 0) | (head == n_head - 1)

    @pl.loop(0, n_head)
    def _(t):
        block = partner(n_head - 1)
        for c in range(n_head - 1):
            block = jnp.where(t == c, partner(c), block)

        @pl.when(block != head)
        def _():
            wait_bytes(q_recv.at[block], zr_sem.at[block])

        for i in range(n_head):
            pl.when(block == i)(functools.partial(attend, i))

        @pl.when((block != head) & end)
        def _():
            @pl.loop(0, jobs)
            def _(j):
                step(block, j)

    @pl.when(jnp.logical_not(end))
    def _():
        @pl.loop(0, n_head - 1)
        def _(t):
            above, below = n_head - 1 - t, t

            @pl.loop(0, jobs)
            def _(j):
                @pl.when(above > head)
                def _():
                    step(above, j)

                @pl.when(below < head)
                def _():
                    step(below, j)

    quarter = cols // 2

    @pl.loop(0, jobs)
    def _(j):
        acc[...] = partial(head, j)

        @pl.when(head > 0)
        def _():
            wait_bytes(s_recv.at[head + 1, j], sr_sem.at[head + 1, j])
            acc[...] += s_recv[head + 1, j].astype(f32)

        @pl.when(head < n_head - 1)
        def _():
            wait_bytes(s_recv.at[head, j], sr_sem.at[head, j])
            acc[...] += s_recv[head, j].astype(f32)

        proj = acc[...].astype(bf16)
        back = (dot(r_one[0], proj[:, :quarter]) + dot(r_one[1], proj[:, quarter:])).astype(bf16)
        b_send[j] = back.reshape(n_seq, 2 * cap, quarter)
        b_recv[j, pl.ds(seq, 1)] = b_send[j, pl.ds(seq, 1)]

        @pl.loop(1, n_seq)
        def _(i):
            peer = (seq + i) % n_seq
            pltpu.make_async_remote_copy(
                src_ref=b_send.at[j, peer], dst_ref=b_recv.at[j, seq],
                send_sem=bs_sem.at[j], recv_sem=br_sem.at[j],
                device_id=(peer, head), device_id_type=MESH,
            ).start()

    for j in range(jobs):
        wait_bytes(b_recv.at[j, pl.ds(0, n_seq - 1)], br_sem.at[j])
        arrived = b_recv[j].reshape(slots, quarter)
        mine = jnp.concatenate([dot(pt_one[0], arrived), dot(pt_one[1], arrived)], axis=1)
        out[:, j * cols : (j + 1) * cols] = mine.astype(bf16)

    wait_bytes(kx_send.at[pl.ds(0, n_seq - 1)], kxs_sem)
    for c in range(n_head):
        wait_bytes(x_send.at[c, pl.ds(0, n_seq - 1)], xs_sem.at[c])
        if c > 0:
            wait_bytes(k_send.at[c], ks_sem.at[c])

        @pl.when(partner(c) != head)
        def _():
            wait_bytes(z_send.at[c], zs_sem.at[c])

    @pl.loop(0, jobs)
    def _(j):
        wait_bytes(b_send.at[j, pl.ds(0, n_seq - 1)], bs_sem.at[j])

        @pl.loop(1, n_head)
        def _(i):
            block = (head + i) % n_head
            wait_bytes(s_send.at[block, j], ss_sem.at[block, j])


def finish(mine, residual, gain, out_res, out_norm):
    f32, bf16 = jnp.float32, jnp.bfloat16
    stream = (residual[...].astype(f32) + mine[...].astype(f32)).astype(bf16)
    out_res[...] = stream
    wide = stream.astype(f32)
    scale = lax.rsqrt(jnp.mean(wide * wide, axis=-1, keepdims=True) + 1e-06)
    out_norm[...] = (wide * scale * gain[...]).astype(bf16)


def local(qkv, residual, dest_row, source_row, doc_start, out_weight, norm_gain):
    n_seq = lax.axis_size("seq")
    n_head = lax.axis_size("head")
    tok, _ = qkv.shape
    depth, model = out_weight.shape
    cap = -(-max(2, 3 * tok // (2 * n_seq)) // 8) * 8
    jobs = 4
    cols = model // jobs
    bf16 = jnp.bfloat16
    dma = pltpu.SemaphoreType.DMA
    vmem = pl.BlockSpec(memory_space=pltpu.VMEM)
    mine = pl.pallas_call(
        functools.partial(kernel, n_seq, n_head, cap, jobs),
        out_shape=jax.ShapeDtypeStruct(residual.shape, bf16),
        in_specs=[vmem, vmem, vmem, vmem, pl.BlockSpec(memory_space=pl.ANY)],
        out_specs=vmem,
        scratch_shapes=[
            pltpu.VMEM((depth, model), bf16),
            pltpu.VMEM((2, n_seq * 2 * cap, tok), bf16),
            pltpu.VMEM((2, tok, n_seq * 2 * cap), bf16),
            pltpu.VMEM((2, n_seq * 2 * cap, tok), bf16),
            pltpu.VMEM((2, tok, n_seq * 2 * cap), bf16),
            pltpu.VMEM((n_seq, 2 * cap, KVH * HD), bf16),
            pltpu.VMEM((n_seq, 2 * cap, KVH * HD), bf16),
            pltpu.VMEM((n_head, n_seq, 2 * cap, depth // 2), bf16),
            pltpu.VMEM((n_head, n_seq, 2 * cap, depth // 2), bf16),
            pltpu.VMEM((tok, 2 * KVH * HD), bf16),
            pltpu.VMEM((n_head, tok, 2 * HD), bf16),
            pltpu.VMEM((n_head, tok, 2 * HD), bf16),
            pltpu.VMEM((n_head, tok, depth), bf16),
            pltpu.VMEM((n_head, tok, depth), bf16),
            pltpu.VMEM((n_head, tok, depth), bf16),
            pltpu.VMEM((n_head, jobs, tok, cols), bf16),
            pltpu.VMEM((n_head + 1, jobs, tok, cols), bf16),
            pltpu.VMEM((tok, cols), jnp.float32),
            pltpu.VMEM((jobs, n_seq, 2 * cap, cols // 2), bf16),
            pltpu.VMEM((jobs, n_seq, 2 * cap, cols // 2), bf16),
            dma,
            dma,
            dma,
            dma((n_head,)),
            dma((n_head,)),
            dma((n_head,)),
            dma((n_head,)),
            dma((n_head,)),
            dma((n_head,)),
            dma((n_head, jobs)),
            dma((n_head + 1, jobs)),
            dma((jobs,)),
            dma((jobs,)),
        ],
        compiler_params=pltpu.CompilerParams(
            collective_id=0, has_side_effects=True, vmem_limit_bytes=56 * 1024 * 1024
        ),
        name="layer",
    )(
        qkv,
        dest_row.reshape(1, tok),
        source_row.reshape(1, tok),
        doc_start.reshape(1, tok * n_head),
        out_weight,
    )
    return pl.pallas_call(
        finish,
        out_shape=(jax.ShapeDtypeStruct(residual.shape, bf16), jax.ShapeDtypeStruct(residual.shape, bf16)),
        compiler_params=pltpu.CompilerParams(vmem_limit_bytes=16 * 1024 * 1024),
        name="finish",
    )(mine, residual, norm_gain.reshape(1, model))


def solution(mesh):
    return jax.shard_map(
        local,
        mesh=mesh,
        in_specs=(
            P(("seq", "head"), None),
            P(("seq", "head"), None),
            P(("seq", "head")),
            P(("seq", "head")),
            P("seq"),
            P("head", None),
            P(),
        ),
        out_specs=(P(("seq", "head"), None), P(("seq", "head"), None)),
        check_vma=False,
    )
```

```python
import functools

import jax
import jax.numpy as jnp
import numpy as np
from jax import lax
from jax.experimental import pallas as pl
from jax.experimental.pallas import tpu as pltpu
from jax.sharding import PartitionSpec as P

QH = 24
KVH = 4
HD = 128
MESH = pl.DeviceIdType.MESH


def one_hot_slots(member, ranks, n_seq, cap):
    rows = member.shape[1]
    rank = jnp.where(member, ranks.astype(jnp.int32), -4 * cap)
    place = lax.broadcasted_iota(jnp.int32, (n_seq, 2 * cap, rows), 1)
    low = (rank[:, None, :] == place).astype(jnp.float32).reshape(n_seq * 2 * cap, rows)
    high = (rank[:, None, :] + cap == place).astype(jnp.float32).reshape(n_seq * 2 * cap, rows)
    return low, high


def kernel(
    n_seq, n_head, cap, jobs,
    qkv, dest, source, starts, weight,
    out,
    w_vmem, p_one, pt_one, r_one, rt_one, kx_send, kx_recv, x_send, x_recv, kv_rows, k_send, kv_recv,
    z_send, q_recv, attn, s_send, s_recv, acc, b_send, b_recv,
    w_sem, kxs_sem, kxr_sem, xs_sem, xr_sem, ks_sem, kr_sem, zs_sem, zr_sem, ss_sem, sr_sem, bs_sem, br_sem,
):
    f32, bf16 = jnp.float32, jnp.bfloat16
    seq, head = lax.axis_index("seq"), lax.axis_index("head")
    tok = qkv.shape[0]
    group = tok * n_head
    heads_here = weight.shape[0] // HD
    shared = QH // KVH
    cols = weight.shape[1] // jobs
    slots = n_seq * 2 * cap

    def dot(a, b):
        return jnp.dot(a, b, preferred_element_type=f32)

    def wait_bytes(ref, sem):
        pltpu.make_async_copy(ref, ref, sem).wait()

    load_w = pltpu.make_async_copy(weight, w_vmem, w_sem)
    load_w.start()

    barrier = pltpu.get_barrier_semaphore()

    @pl.loop(1, n_seq)
    def _(i):
        pl.semaphore_signal(barrier, inc=1, device_id=((seq + i) % n_seq, head), device_id_type=MESH)

    @pl.loop(1, n_head)
    def _(i):
        pl.semaphore_signal(barrier, inc=1, device_id=(seq, (head + i) % n_head), device_id_type=MESH)

    bounds = lax.broadcasted_iota(jnp.int32, (n_seq, tok), 0) * group
    goes = (dest[...] >= bounds) & (dest[...] < bounds + group)
    comes = (source[...] >= bounds) & (source[...] < bounds + group)
    earlier = lax.broadcasted_iota(jnp.int32, (tok, tok), 0) < lax.broadcasted_iota(jnp.int32, (tok, tok), 1)
    low, high = one_hot_slots(goes, dot(goes.astype(f32).astype(bf16), earlier.astype(f32).astype(bf16)), n_seq, cap)
    p_one[0], p_one[1] = low.astype(bf16), high.astype(bf16)

    pl.semaphore_wait(barrier, n_seq + n_head - 2)

    def partner(c):
        if n_head == 4:
            mirror = n_head - 1 - head
            return [mirror, (head + 2) % n_head, (mirror + 2) % n_head, head][c]
        return (shifts[c] - head + n_head) % n_head

    def place(x, send, recv, s_sem, r_sem):
        side = x.shape[1] // 2
        placed = (dot(p_one[0], x[:, :side]) + dot(p_one[1], x[:, side:])).astype(bf16)
        send[...] = placed.reshape(n_seq, 2 * cap, side)
        recv[pl.ds(seq, 1)] = send[pl.ds(seq, 1)]

        @pl.loop(1, n_seq)
        def _(i):
            peer = (seq + i) % n_seq
            pltpu.make_async_remote_copy(
                src_ref=send.at[peer], dst_ref=recv.at[seq],
                send_sem=s_sem, recv_sem=r_sem,
                device_id=(peer, head), device_id_type=MESH,
            ).start()

    def gather(recv, r_sem):
        wait_bytes(recv.at[pl.ds(0, n_seq - 1)], r_sem)
        arrived = recv[...].reshape(slots, recv.shape[2])
        return jnp.concatenate([dot(rt_one[0], arrived), dot(rt_one[1], arrived)], axis=1).astype(bf16)

    shifts = [(n_head - 1 + c) % n_head for c in range(n_head)]
    depth = heads_here * HD
    place(qkv[:, QH * HD :], kx_send, kx_recv, kxs_sem, kxr_sem)

    low_t, high_t = low.T, high.T
    pt_one[0], pt_one[1] = low_t.astype(bf16), high_t.astype(bf16)
    across = jnp.broadcast_to(source[...].astype(f32), (tok, tok))
    before = (across.T < across).astype(f32).astype(bf16)
    rlow, rhigh = one_hot_slots(comes, dot(comes.astype(f32).astype(bf16), before), n_seq, cap)
    r_one[0], r_one[1] = rlow.astype(bf16), rhigh.astype(bf16)
    rt_one[0], rt_one[1] = rlow.T.astype(bf16), rhigh.T.astype(bf16)

    def place_query(c):
        query = qkv[:, pl.ds(pl.multiple_of(partner(c) * depth, HD), depth)]
        place(query, x_send.at[c], x_recv.at[c], xs_sem.at[c], xr_sem.at[c])

    place_query(0)
    kv_rows[...] = gather(kx_recv, kxr_sem)

    def kv_of(block):
        kv = (block * heads_here) // shared
        key = kv_rows[:, pl.ds(pl.multiple_of(kv * HD, HD), HD)]
        value = kv_rows[:, pl.ds(pl.multiple_of((KVH + kv) * HD, HD), HD)]
        return jnp.concatenate([key, value], axis=1)

    kv_recv[pl.ds(head, 1)] = kv_of(head)[None]
    for c in range(1, n_head):
        to = (head + c) % n_head
        k_send[c] = kv_of(to)
        pltpu.make_async_remote_copy(
            src_ref=k_send.at[c], dst_ref=kv_recv.at[head],
            send_sem=ks_sem.at[c], recv_sem=kr_sem.at[head],
            device_id=(seq, to), device_id_type=MESH,
        ).start()

    for c in range(n_head):
        if c + 1 < n_head:
            place_query(c + 1)
        rows = gather(x_recv.at[c], xr_sem.at[c])
        to = partner(c)
        z_send[c] = rows

        @pl.when(to == head)
        def _():
            q_recv[pl.ds(head, 1)] = z_send[pl.ds(c, 1)]

        @pl.when(to != head)
        def _():
            pltpu.make_async_remote_copy(
                src_ref=z_send.at[c], dst_ref=q_recv.at[head],
                send_sem=zs_sem.at[c], recv_sem=zr_sem.at[head],
                device_id=(seq, to), device_id_type=MESH,
            ).start()

    @pl.loop(1, n_head)
    def _(i):
        other = (head + i) % n_head
        wait_bytes(kv_recv.at[other], kr_sem.at[other])

    load_w.wait()
    factor = HD ** (-0.5) * float(np.log2(np.e))

    def attend(i):
        span = (i + 1) * tok
        keys = kv_recv[: i + 1, :, :HD].reshape(span, HD)
        values = kv_recv[: i + 1, :, HD:].reshape(span, HD)
        first = jnp.broadcast_to(starts[:, i * tok : (i + 1) * tok].astype(f32), (tok, tok)).T[:, :1]
        kplace = lax.broadcasted_iota(jnp.int32, (tok, span), 1)
        qplace = lax.broadcasted_iota(jnp.int32, (tok, span), 0) + i * tok
        visible = (kplace <= qplace) & (kplace >= first.astype(jnp.int32))
        for a in range(heads_here):
            scores = lax.dot_general(
                q_recv[i, :, a * HD : (a + 1) * HD], keys, (((1,), (1,)), ((), ())), preferred_element_type=f32
            )
            scores = jnp.where(visible, scores, -1e30)
            top = jnp.max(scores, axis=-1, keepdims=True)
            weights = jnp.exp2((scores - top) * factor)
            total = jnp.sum(weights, axis=-1, keepdims=True)
            attn[i, :, a * HD : (a + 1) * HD] = (dot(weights.astype(bf16), values) / total).astype(bf16)

    def partial(block, j):
        return dot(attn[block], w_vmem[:, pl.ds(pl.multiple_of(j * cols, cols), cols)])

    def step(block, j):
        up = block > head
        slot = jnp.where(up, block + 1, block)
        acc[...] = partial(block, j)

        @pl.when((head > 0) & (head < n_head - 1))
        def _():
            wait_bytes(s_recv.at[slot, j], sr_sem.at[slot, j])
            acc[...] += s_recv[slot, j].astype(f32)

        s_send[block, j] = acc[...].astype(bf16)
        pltpu.make_async_remote_copy(
            src_ref=s_send.at[block, j], dst_ref=s_recv.at[slot, j],
            send_sem=ss_sem.at[block, j], recv_sem=sr_sem.at[slot, j],
            device_id=(seq, jnp.where(up, head + 1, head - 1)), device_id_type=MESH,
        ).start()

    end = (head == 0) | (head == n_head - 1)

    def chain(block):
        @pl.loop(0, jobs)
        def _(j):
            step(block, j)

    order = [0, n_head - 1] + list(range(1, n_head - 1))

    @pl.loop(0, n_head)
    def _(t):
        block = partner(order[0])
        for place_in, c in enumerate(order):
            block = jnp.where(t == place_in, partner(c), block)

        @pl.when(block != head)
        def _():
            wait_bytes(q_recv.at[block], zr_sem.at[block])

        for i in range(n_head):
            pl.when(block == i)(functools.partial(attend, i))

        @pl.when((block != head) & end)
        def _():
            chain(block)

        if n_head == 4:

            @pl.when(jnp.logical_not(end) & (t == 2))
            def _():
                chain(partner(1))
                chain(partner(0))

            @pl.when(jnp.logical_not(end) & (t == 3))
            def _():
                chain(partner(2))

    if n_head != 4:

        @pl.when(jnp.logical_not(end))
        def _():
            @pl.loop(0, n_head - 1)
            def _(t):
                above, below = n_head - 1 - t, t

                @pl.loop(0, jobs)
                def _(j):
                    @pl.when(above > head)
                    def _():
                        step(above, j)

                    @pl.when(below < head)
                    def _():
                        step(below, j)

    quarter = cols // 2

    @pl.loop(0, jobs)
    def _(j):
        acc[...] = partial(head, j)

        @pl.when(head > 0)
        def _():
            wait_bytes(s_recv.at[head + 1, j], sr_sem.at[head + 1, j])
            acc[...] += s_recv[head + 1, j].astype(f32)

        @pl.when(head < n_head - 1)
        def _():
            wait_bytes(s_recv.at[head, j], sr_sem.at[head, j])
            acc[...] += s_recv[head, j].astype(f32)

        proj = acc[...].astype(bf16)
        back = (dot(r_one[0], proj[:, :quarter]) + dot(r_one[1], proj[:, quarter:])).astype(bf16)
        b_send[j] = back.reshape(n_seq, 2 * cap, quarter)
        b_recv[j, pl.ds(seq, 1)] = b_send[j, pl.ds(seq, 1)]

        @pl.loop(1, n_seq)
        def _(i):
            peer = (seq + i) % n_seq
            pltpu.make_async_remote_copy(
                src_ref=b_send.at[j, peer], dst_ref=b_recv.at[j, seq],
                send_sem=bs_sem.at[j], recv_sem=br_sem.at[j],
                device_id=(peer, head), device_id_type=MESH,
            ).start()

    for j in range(jobs):
        wait_bytes(b_recv.at[j, pl.ds(0, n_seq - 1)], br_sem.at[j])
        arrived = b_recv[j].reshape(slots, quarter)
        mine = jnp.concatenate([dot(pt_one[0], arrived), dot(pt_one[1], arrived)], axis=1)
        out[:, j * cols : (j + 1) * cols] = mine.astype(bf16)

    wait_bytes(kx_send.at[pl.ds(0, n_seq - 1)], kxs_sem)
    for c in range(n_head):
        wait_bytes(x_send.at[c, pl.ds(0, n_seq - 1)], xs_sem.at[c])
        if c > 0:
            wait_bytes(k_send.at[c], ks_sem.at[c])

        @pl.when(partner(c) != head)
        def _():
            wait_bytes(z_send.at[c], zs_sem.at[c])

    @pl.loop(0, jobs)
    def _(j):
        wait_bytes(b_send.at[j, pl.ds(0, n_seq - 1)], bs_sem.at[j])

        @pl.loop(1, n_head)
        def _(i):
            block = (head + i) % n_head
            wait_bytes(s_send.at[block, j], ss_sem.at[block, j])


def finish(mine, residual, gain, out_res, out_norm):
    f32, bf16 = jnp.float32, jnp.bfloat16
    stream = (residual[...].astype(f32) + mine[...].astype(f32)).astype(bf16)
    out_res[...] = stream
    wide = stream.astype(f32)
    scale = lax.rsqrt(jnp.mean(wide * wide, axis=-1, keepdims=True) + 1e-06)
    out_norm[...] = (wide * scale * gain[...]).astype(bf16)


def local(qkv, residual, dest_row, source_row, doc_start, out_weight, norm_gain):
    n_seq = lax.axis_size("seq")
    n_head = lax.axis_size("head")
    tok, _ = qkv.shape
    depth, model = out_weight.shape
    cap = -(-max(2, 3 * tok // (2 * n_seq)) // 8) * 8
    jobs = 4
    cols = model // jobs
    bf16 = jnp.bfloat16
    dma = pltpu.SemaphoreType.DMA
    vmem = pl.BlockSpec(memory_space=pltpu.VMEM)
    mine = pl.pallas_call(
        functools.partial(kernel, n_seq, n_head, cap, jobs),
        out_shape=jax.ShapeDtypeStruct(residual.shape, bf16),
        in_specs=[vmem, vmem, vmem, vmem, pl.BlockSpec(memory_space=pl.ANY)],
        out_specs=vmem,
        scratch_shapes=[
            pltpu.VMEM((depth, model), bf16),
            pltpu.VMEM((2, n_seq * 2 * cap, tok), bf16),
            pltpu.VMEM((2, tok, n_seq * 2 * cap), bf16),
            pltpu.VMEM((2, n_seq * 2 * cap, tok), bf16),
            pltpu.VMEM((2, tok, n_seq * 2 * cap), bf16),
            pltpu.VMEM((n_seq, 2 * cap, KVH * HD), bf16),
            pltpu.VMEM((n_seq, 2 * cap, KVH * HD), bf16),
            pltpu.VMEM((n_head, n_seq, 2 * cap, depth // 2), bf16),
            pltpu.VMEM((n_head, n_seq, 2 * cap, depth // 2), bf16),
            pltpu.VMEM((tok, 2 * KVH * HD), bf16),
            pltpu.VMEM((n_head, tok, 2 * HD), bf16),
            pltpu.VMEM((n_head, tok, 2 * HD), bf16),
            pltpu.VMEM((n_head, tok, depth), bf16),
            pltpu.VMEM((n_head, tok, depth), bf16),
            pltpu.VMEM((n_head, tok, depth), bf16),
            pltpu.VMEM((n_head, jobs, tok, cols), bf16),
            pltpu.VMEM((n_head + 1, jobs, tok, cols), bf16),
            pltpu.VMEM((tok, cols), jnp.float32),
            pltpu.VMEM((jobs, n_seq, 2 * cap, cols // 2), bf16),
            pltpu.VMEM((jobs, n_seq, 2 * cap, cols // 2), bf16),
            dma,
            dma,
            dma,
            dma((n_head,)),
            dma((n_head,)),
            dma((n_head,)),
            dma((n_head,)),
            dma((n_head,)),
            dma((n_head,)),
            dma((n_head, jobs)),
            dma((n_head + 1, jobs)),
            dma((jobs,)),
            dma((jobs,)),
        ],
        compiler_params=pltpu.CompilerParams(
            collective_id=0, has_side_effects=True, vmem_limit_bytes=56 * 1024 * 1024
        ),
        name="layer",
    )(
        qkv,
        dest_row.reshape(1, tok),
        source_row.reshape(1, tok),
        doc_start.reshape(1, tok * n_head),
        out_weight,
    )
    return pl.pallas_call(
        finish,
        out_shape=(jax.ShapeDtypeStruct(residual.shape, bf16), jax.ShapeDtypeStruct(residual.shape, bf16)),
        compiler_params=pltpu.CompilerParams(vmem_limit_bytes=16 * 1024 * 1024),
        name="finish",
    )(mine, residual, norm_gain.reshape(1, model))


def solution(mesh):
    return jax.shard_map(
        local,
        mesh=mesh,
        in_specs=(
            P(("seq", "head"), None),
            P(("seq", "head"), None),
            P(("seq", "head")),
            P(("seq", "head")),
            P("seq"),
            P("head", None),
            P(),
        ),
        out_specs=(P(("seq", "head"), None), P(("seq", "head"), None)),
        check_vma=False,
    )
```

```python
import functools

import jax
import jax.numpy as jnp
import numpy as np
from jax import lax
from jax.experimental import pallas as pl
from jax.experimental.pallas import tpu as pltpu
from jax.sharding import PartitionSpec as P

QH = 24
KVH = 4
HD = 128
MESH = pl.DeviceIdType.MESH


def one_hot_slots(member, ranks, n_seq, cap):
    rows = member.shape[1]
    rank = jnp.where(member, ranks.astype(jnp.int32), -4 * cap)
    place = lax.broadcasted_iota(jnp.int32, (n_seq, 2 * cap, rows), 1)
    low = (rank[:, None, :] == place).astype(jnp.float32).reshape(n_seq * 2 * cap, rows)
    high = (rank[:, None, :] + cap == place).astype(jnp.float32).reshape(n_seq * 2 * cap, rows)
    return low, high


def kernel(
    n_seq, n_head, cap, jobs,
    qkv_hbm, dest, source, starts, weight,
    out,
    qkv, w_vmem, p_one, pt_one, r_one, rt_one, kx_send, kx_recv, x_send, x_recv, kv_rows, k_send, kv_recv,
    z_send, q_recv, attn, s_send, s_recv, acc, b_send, b_recv,
    in_sem, w_sem, kxs_sem, kxr_sem, xs_sem, xr_sem, ks_sem, kr_sem, zs_sem, zr_sem, ss_sem, sr_sem, bs_sem, br_sem,
):
    f32, bf16 = jnp.float32, jnp.bfloat16
    seq, head = lax.axis_index("seq"), lax.axis_index("head")
    tok = qkv.shape[0]
    group = tok * n_head
    heads_here = weight.shape[0] // HD
    shared = QH // KVH
    cols = weight.shape[1] // jobs
    slots = n_seq * 2 * cap

    def dot(a, b):
        return jnp.dot(a, b, preferred_element_type=f32)

    def wait_bytes(ref, sem):
        pltpu.make_async_copy(ref, ref, sem).wait()

    loads = [
        pltpu.make_async_copy(qkv_hbm.at[:, part], qkv.at[:, part], in_sem.at[at])
        for at, part in enumerate((slice(QH * HD, None), slice(0, QH * HD)))
    ]
    for load in loads:
        load.start()
    load_w = pltpu.make_async_copy(weight, w_vmem, w_sem)

    barrier = pltpu.get_barrier_semaphore()

    @pl.loop(1, n_seq)
    def _(i):
        pl.semaphore_signal(barrier, inc=1, device_id=((seq + i) % n_seq, head), device_id_type=MESH)

    @pl.loop(1, n_head)
    def _(i):
        pl.semaphore_signal(barrier, inc=1, device_id=(seq, (head + i) % n_head), device_id_type=MESH)

    bounds = lax.broadcasted_iota(jnp.int32, (n_seq, tok), 0) * group
    goes = (dest[...] >= bounds) & (dest[...] < bounds + group)
    comes = (source[...] >= bounds) & (source[...] < bounds + group)
    earlier = lax.broadcasted_iota(jnp.int32, (tok, tok), 0) < lax.broadcasted_iota(jnp.int32, (tok, tok), 1)
    low, high = one_hot_slots(goes, dot(goes.astype(f32).astype(bf16), earlier.astype(f32).astype(bf16)), n_seq, cap)
    p_one[0], p_one[1] = low.astype(bf16), high.astype(bf16)

    pl.semaphore_wait(barrier, n_seq + n_head - 2)

    def partner(c):
        if n_head == 4:
            mirror = n_head - 1 - head
            return [mirror, (head + 2) % n_head, (mirror + 2) % n_head, head][c]
        return (shifts[c] - head + n_head) % n_head

    def place(x, send, recv, s_sem, r_sem):
        side = x.shape[1] // 2
        placed = (dot(p_one[0], x[:, :side]) + dot(p_one[1], x[:, side:])).astype(bf16)
        send[...] = placed.reshape(n_seq, 2 * cap, side)
        recv[pl.ds(seq, 1)] = send[pl.ds(seq, 1)]

        @pl.loop(1, n_seq)
        def _(i):
            peer = (seq + i) % n_seq
            pltpu.make_async_remote_copy(
                src_ref=send.at[peer], dst_ref=recv.at[seq],
                send_sem=s_sem, recv_sem=r_sem,
                device_id=(peer, head), device_id_type=MESH,
            ).start()

    def gather(recv, r_sem):
        wait_bytes(recv.at[pl.ds(0, n_seq - 1)], r_sem)
        arrived = recv[...].reshape(slots, recv.shape[2])
        return jnp.concatenate([dot(rt_one[0], arrived), dot(rt_one[1], arrived)], axis=1).astype(bf16)

    shifts = [(n_head - 1 + c) % n_head for c in range(n_head)]
    depth = heads_here * HD
    loads[0].wait()
    place(qkv[:, QH * HD :], kx_send, kx_recv, kxs_sem, kxr_sem)

    low_t, high_t = low.T, high.T
    pt_one[0], pt_one[1] = low_t.astype(bf16), high_t.astype(bf16)
    across = jnp.broadcast_to(source[...].astype(f32), (tok, tok))
    before = (across.T < across).astype(f32).astype(bf16)
    rlow, rhigh = one_hot_slots(comes, dot(comes.astype(f32).astype(bf16), before), n_seq, cap)
    r_one[0], r_one[1] = rlow.astype(bf16), rhigh.astype(bf16)
    rt_one[0], rt_one[1] = rlow.T.astype(bf16), rhigh.T.astype(bf16)

    def place_query(c):
        query = qkv[:, pl.ds(pl.multiple_of(partner(c) * depth, HD), depth)]
        place(query, x_send.at[c], x_recv.at[c], xs_sem.at[c], xr_sem.at[c])

    loads[1].wait()
    load_w.start()
    place_query(0)
    kv_rows[...] = gather(kx_recv, kxr_sem)

    def kv_of(block):
        kv = (block * heads_here) // shared
        key = kv_rows[:, pl.ds(pl.multiple_of(kv * HD, HD), HD)]
        value = kv_rows[:, pl.ds(pl.multiple_of((KVH + kv) * HD, HD), HD)]
        return jnp.concatenate([key, value], axis=1)

    kv_recv[pl.ds(head, 1)] = kv_of(head)[None]
    for c in range(1, n_head):
        to = (head + c) % n_head
        k_send[c] = kv_of(to)
        pltpu.make_async_remote_copy(
            src_ref=k_send.at[c], dst_ref=kv_recv.at[head],
            send_sem=ks_sem.at[c], recv_sem=kr_sem.at[head],
            device_id=(seq, to), device_id_type=MESH,
        ).start()

    for c in range(n_head):
        if c + 1 < n_head:
            place_query(c + 1)
        rows = gather(x_recv.at[c], xr_sem.at[c])
        to = partner(c)
        z_send[c] = rows

        @pl.when(to == head)
        def _():
            q_recv[pl.ds(head, 1)] = z_send[pl.ds(c, 1)]

        @pl.when(to != head)
        def _():
            pltpu.make_async_remote_copy(
                src_ref=z_send.at[c], dst_ref=q_recv.at[head],
                send_sem=zs_sem.at[c], recv_sem=zr_sem.at[head],
                device_id=(seq, to), device_id_type=MESH,
            ).start()

    @pl.loop(1, n_head)
    def _(i):
        other = (head + i) % n_head
        wait_bytes(kv_recv.at[other], kr_sem.at[other])

    load_w.wait()
    factor = HD ** (-0.5) * float(np.log2(np.e))

    def attend(i):
        span = (i + 1) * tok
        keys = kv_recv[: i + 1, :, :HD].reshape(span, HD)
        values = kv_recv[: i + 1, :, HD:].reshape(span, HD)
        first = jnp.broadcast_to(starts[:, i * tok : (i + 1) * tok].astype(f32), (tok, tok)).T[:, :1]
        kplace = lax.broadcasted_iota(jnp.int32, (tok, span), 1)
        qplace = lax.broadcasted_iota(jnp.int32, (tok, span), 0) + i * tok
        visible = (kplace <= qplace) & (kplace >= first.astype(jnp.int32))
        for a in range(heads_here):
            scores = lax.dot_general(
                q_recv[i, :, a * HD : (a + 1) * HD], keys, (((1,), (1,)), ((), ())), preferred_element_type=f32
            )
            scores = jnp.where(visible, scores, -1e30)
            top = jnp.max(scores, axis=-1, keepdims=True)
            weights = jnp.exp2((scores - top) * factor)
            total = jnp.sum(weights, axis=-1, keepdims=True)
            attn[i, :, a * HD : (a + 1) * HD] = (dot(weights.astype(bf16), values) / total).astype(bf16)

    def partial(block, j):
        return dot(attn[block], w_vmem[:, pl.ds(pl.multiple_of(j * cols, cols), cols)])

    def step(block, j):
        up = block > head
        slot = jnp.where(up, block + 1, block)
        acc[...] = partial(block, j)

        @pl.when((head > 0) & (head < n_head - 1))
        def _():
            wait_bytes(s_recv.at[slot, j], sr_sem.at[slot, j])
            acc[...] += s_recv[slot, j].astype(f32)

        s_send[block, j] = acc[...].astype(bf16)
        pltpu.make_async_remote_copy(
            src_ref=s_send.at[block, j], dst_ref=s_recv.at[slot, j],
            send_sem=ss_sem.at[block, j], recv_sem=sr_sem.at[slot, j],
            device_id=(seq, jnp.where(up, head + 1, head - 1)), device_id_type=MESH,
        ).start()

    end = (head == 0) | (head == n_head - 1)

    def chain(block):
        @pl.loop(0, jobs)
        def _(j):
            step(block, j)

    quarter = cols // 2

    def own(j):
        acc[...] = partial(head, j)

        @pl.when(head > 0)
        def _():
            wait_bytes(s_recv.at[head + 1, j], sr_sem.at[head + 1, j])
            acc[...] += s_recv[head + 1, j].astype(f32)

        @pl.when(head < n_head - 1)
        def _():
            wait_bytes(s_recv.at[head, j], sr_sem.at[head, j])
            acc[...] += s_recv[head, j].astype(f32)

        proj = acc[...].astype(bf16)
        back = (dot(r_one[0], proj[:, :quarter]) + dot(r_one[1], proj[:, quarter:])).astype(bf16)
        b_send[j] = back.reshape(n_seq, 2 * cap, quarter)
        b_recv[j, pl.ds(seq, 1)] = b_send[j, pl.ds(seq, 1)]

        @pl.loop(1, n_seq)
        def _(i):
            peer = (seq + i) % n_seq
            pltpu.make_async_remote_copy(
                src_ref=b_send.at[j, peer], dst_ref=b_recv.at[j, seq],
                send_sem=bs_sem.at[j], recv_sem=br_sem.at[j],
                device_id=(peer, head), device_id_type=MESH,
            ).start()

    def paced(c, j):
        older = partner(c) if c == 0 else jnp.where(j >= 2, partner(c), partner(c - 1))
        at = (j + jobs - 2) % jobs
        wait_bytes(s_send.at[older, at], ss_sem.at[older, at])
        step(partner(c), j)

    order = [0, n_head - 1] + list(range(1, n_head - 1))

    @pl.loop(0, n_head)
    def _(t):
        block = partner(order[0])
        for place_in, c in enumerate(order):
            block = jnp.where(t == place_in, partner(c), block)

        @pl.when(block != head)
        def _():
            wait_bytes(q_recv.at[block], zr_sem.at[block])

        for i in range(n_head):
            pl.when(block == i)(functools.partial(attend, i))

        if n_head != 4:

            @pl.when((block != head) & end)
            def _():
                chain(block)
        else:

            @pl.when(end & (t == 0))
            def _():
                @pl.loop(0, 2)
                def _(j):
                    step(partner(0), j)

            @pl.when(end & (t == 1))
            def _():
                @pl.loop(2, jobs)
                def _(j):
                    paced(0, j)

            @pl.when(end & (t == 2))
            def _():
                @pl.loop(0, 2)
                def _(j):
                    paced(1, j)

    if n_head == 4:

        @pl.when(end)
        def _():
            @pl.loop(2, jobs)
            def _(j):
                paced(1, j)

            @pl.loop(0, jobs)
            def _(j):
                paced(2, j)
                own(j)

        @pl.when(jnp.logical_not(end))
        def _():
            @pl.loop(0, jobs)
            def _(j):
                step(partner(1), j)
                step(partner(2), j)

            chain(partner(0))

            @pl.loop(0, jobs)
            def _(j):
                own(j)

    else:

        @pl.when(jnp.logical_not(end))
        def _():
            @pl.loop(0, n_head - 1)
            def _(t):
                above, below = n_head - 1 - t, t

                @pl.loop(0, jobs)
                def _(j):
                    @pl.when(above > head)
                    def _():
                        step(above, j)

                    @pl.when(below < head)
                    def _():
                        step(below, j)

        @pl.loop(0, jobs)
        def _(j):
            own(j)

    for j in range(jobs):
        wait_bytes(b_recv.at[j, pl.ds(0, n_seq - 1)], br_sem.at[j])
        arrived = b_recv[j].reshape(slots, quarter)
        mine = jnp.concatenate([dot(pt_one[0], arrived), dot(pt_one[1], arrived)], axis=1)
        out[:, j * cols : (j + 1) * cols] = mine.astype(bf16)

    wait_bytes(kx_send.at[pl.ds(0, n_seq - 1)], kxs_sem)
    for c in range(n_head):
        wait_bytes(x_send.at[c, pl.ds(0, n_seq - 1)], xs_sem.at[c])
        if c > 0:
            wait_bytes(k_send.at[c], ks_sem.at[c])

        @pl.when(partner(c) != head)
        def _():
            wait_bytes(z_send.at[c], zs_sem.at[c])

    @pl.loop(0, jobs)
    def _(j):
        wait_bytes(b_send.at[j, pl.ds(0, n_seq - 1)], bs_sem.at[j])

        @pl.loop(1, n_head)
        def _(i):
            block = (head + i) % n_head
            left = (block == partner(n_head - 2)) & (j >= jobs - 2) if n_head == 4 else block != head

            @pl.when(jnp.logical_not(end) | left)
            def _():
                wait_bytes(s_send.at[block, j], ss_sem.at[block, j])


def finish(mine, residual, gain, out_res, out_norm):
    f32, bf16 = jnp.float32, jnp.bfloat16
    stream = (residual[...].astype(f32) + mine[...].astype(f32)).astype(bf16)
    out_res[...] = stream
    wide = stream.astype(f32)
    scale = lax.rsqrt(jnp.mean(wide * wide, axis=-1, keepdims=True) + 1e-06)
    out_norm[...] = (wide * scale * gain[...]).astype(bf16)


def local(qkv, residual, dest_row, source_row, doc_start, out_weight, norm_gain):
    n_seq = lax.axis_size("seq")
    n_head = lax.axis_size("head")
    tok, _ = qkv.shape
    depth, model = out_weight.shape
    cap = -(-max(2, 3 * tok // (2 * n_seq)) // 8) * 8
    jobs = 4
    cols = model // jobs
    bf16 = jnp.bfloat16
    dma = pltpu.SemaphoreType.DMA
    vmem = pl.BlockSpec(memory_space=pltpu.VMEM)
    hbm = pl.BlockSpec(memory_space=pltpu.HBM)
    scratch = [
        pltpu.VMEM(qkv.shape, bf16),
        pltpu.VMEM((depth, model), bf16),
        pltpu.VMEM((2, n_seq * 2 * cap, tok), bf16),
        pltpu.VMEM((2, tok, n_seq * 2 * cap), bf16),
        pltpu.VMEM((2, n_seq * 2 * cap, tok), bf16),
        pltpu.VMEM((2, tok, n_seq * 2 * cap), bf16),
        pltpu.VMEM((n_seq, 2 * cap, KVH * HD), bf16),
        pltpu.VMEM((n_seq, 2 * cap, KVH * HD), bf16),
        pltpu.VMEM((n_head, n_seq, 2 * cap, depth // 2), bf16),
        pltpu.VMEM((n_head, n_seq, 2 * cap, depth // 2), bf16),
        pltpu.VMEM((tok, 2 * KVH * HD), bf16),
        pltpu.VMEM((n_head, tok, 2 * HD), bf16),
        pltpu.VMEM((n_head, tok, 2 * HD), bf16),
        pltpu.VMEM((n_head, tok, depth), bf16),
        pltpu.VMEM((n_head, tok, depth), bf16),
        pltpu.VMEM((n_head, tok, depth), bf16),
        pltpu.VMEM((n_head, jobs, tok, cols), bf16),
        pltpu.VMEM((n_head + 1, jobs, tok, cols), bf16),
        pltpu.VMEM((tok, cols), jnp.float32),
        pltpu.VMEM((jobs, n_seq, 2 * cap, cols // 2), bf16),
        pltpu.VMEM((jobs, n_seq, 2 * cap, cols // 2), bf16),
        dma((2,)),
        dma,
        dma,
        dma,
        dma((n_head,)),
        dma((n_head,)),
        dma((n_head,)),
        dma((n_head,)),
        dma((n_head,)),
        dma((n_head,)),
        dma((n_head, jobs)),
        dma((n_head + 1, jobs)),
        dma((jobs,)),
        dma((jobs,)),
    ]
    mine = pl.pallas_call(
        functools.partial(kernel, n_seq, n_head, cap, jobs),
        out_shape=jax.ShapeDtypeStruct(residual.shape, bf16),
        in_specs=[hbm, vmem, vmem, vmem, hbm],
        out_specs=vmem,
        scratch_shapes=scratch,
        compiler_params=pltpu.CompilerParams(
            collective_id=0, has_side_effects=True, vmem_limit_bytes=56 * 1024 * 1024
        ),
        name="layer",
    )(
        qkv,
        dest_row.reshape(1, tok),
        source_row.reshape(1, tok),
        doc_start.reshape(1, tok * n_head),
        out_weight,
    )
    return pl.pallas_call(
        finish,
        out_shape=(jax.ShapeDtypeStruct(residual.shape, bf16), jax.ShapeDtypeStruct(residual.shape, bf16)),
        compiler_params=pltpu.CompilerParams(vmem_limit_bytes=16 * 1024 * 1024),
        name="finish",
    )(mine, residual, norm_gain.reshape(1, model))


def solution(mesh):
    return jax.shard_map(
        local,
        mesh=mesh,
        in_specs=(
            P(("seq", "head"), None),
            P(("seq", "head"), None),
            P(("seq", "head")),
            P(("seq", "head")),
            P("seq"),
            P("head", None),
            P(),
        ),
        out_specs=(P(("seq", "head"), None), P(("seq", "head"), None)),
        check_vma=False,
    )
```

```python
import functools

import jax
import jax.numpy as jnp
import numpy as np
from jax import lax
from jax.experimental import pallas as pl
from jax.experimental.pallas import tpu as pltpu
from jax.sharding import PartitionSpec as P

QH = 24
KVH = 4
HD = 128
MESH = pl.DeviceIdType.MESH


def one_hot_slots(member, ranks, n_seq, cap):
    rows = member.shape[1]
    rank = jnp.where(member, ranks.astype(jnp.int32), -4 * cap)
    place = lax.broadcasted_iota(jnp.int32, (n_seq, 2 * cap, rows), 1)
    low = (rank[:, None, :] == place).astype(jnp.float32).reshape(n_seq * 2 * cap, rows)
    high = (rank[:, None, :] + cap == place).astype(jnp.float32).reshape(n_seq * 2 * cap, rows)
    return low, high


def kernel(
    n_seq, n_head, cap, jobs,
    qkv_hbm, dest, source, starts, weight,
    out,
    qkv, w_vmem, p_one, pt_one, r_one, rt_one, kx_send, kx_recv, x_send, x_recv, kv_rows, k_send, kv_recv,
    z_send, q_recv, attn, s_send, s_recv, acc, b_send, b_recv,
    in_sem, w_sem, kxs_sem, kxr_sem, xs_sem, xr_sem, ks_sem, kr_sem, zs_sem, zr_sem, ss_sem, sr_sem, bs_sem, br_sem,
):
    f32, bf16 = jnp.float32, jnp.bfloat16
    seq, head = lax.axis_index("seq"), lax.axis_index("head")
    tok = qkv.shape[0]
    group = tok * n_head
    heads_here = weight.shape[0] // HD
    shared = QH // KVH
    cols = weight.shape[1] // jobs
    slots = n_seq * 2 * cap

    def dot(a, b):
        return jnp.dot(a, b, preferred_element_type=f32)

    def wait_bytes(ref, sem):
        pltpu.make_async_copy(ref, ref, sem).wait()

    loads = [
        pltpu.make_async_copy(qkv_hbm.at[:, part], qkv.at[:, part], in_sem.at[at])
        for at, part in enumerate((slice(QH * HD, None), slice(0, QH * HD)))
    ]
    for load in loads:
        load.start()
    load_w = pltpu.make_async_copy(weight, w_vmem, w_sem)

    barrier = pltpu.get_barrier_semaphore()

    @pl.loop(1, n_seq)
    def _(i):
        pl.semaphore_signal(barrier, inc=1, device_id=((seq + i) % n_seq, head), device_id_type=MESH)

    @pl.loop(1, n_head)
    def _(i):
        pl.semaphore_signal(barrier, inc=1, device_id=(seq, (head + i) % n_head), device_id_type=MESH)

    bounds = lax.broadcasted_iota(jnp.int32, (n_seq, tok), 0) * group
    goes = (dest[...] >= bounds) & (dest[...] < bounds + group)
    comes = (source[...] >= bounds) & (source[...] < bounds + group)
    earlier = lax.broadcasted_iota(jnp.int32, (tok, tok), 0) < lax.broadcasted_iota(jnp.int32, (tok, tok), 1)
    low, high = one_hot_slots(goes, dot(goes.astype(f32).astype(bf16), earlier.astype(f32).astype(bf16)), n_seq, cap)
    p_one[0], p_one[1] = low.astype(bf16), high.astype(bf16)

    pl.semaphore_wait(barrier, n_seq + n_head - 2)

    def partner(c):
        if n_head == 4:
            mirror = n_head - 1 - head
            return [(mirror + 2) % n_head, mirror, (head + 2) % n_head, head][c]
        return (shifts[c] - head + n_head) % n_head

    def place(x, send, recv, s_sem, r_sem):
        side = x.shape[1] // 2
        placed = (dot(p_one[0], x[:, :side]) + dot(p_one[1], x[:, side:])).astype(bf16)
        send[...] = placed.reshape(n_seq, 2 * cap, side)
        recv[pl.ds(seq, 1)] = send[pl.ds(seq, 1)]

        @pl.loop(1, n_seq)
        def _(i):
            peer = (seq + i) % n_seq
            pltpu.make_async_remote_copy(
                src_ref=send.at[peer], dst_ref=recv.at[seq],
                send_sem=s_sem, recv_sem=r_sem,
                device_id=(peer, head), device_id_type=MESH,
            ).start()

    def gather(recv, r_sem):
        wait_bytes(recv.at[pl.ds(0, n_seq - 1)], r_sem)
        arrived = recv[...].reshape(slots, recv.shape[2])
        return jnp.concatenate([dot(rt_one[0], arrived), dot(rt_one[1], arrived)], axis=1).astype(bf16)

    shifts = [(n_head - 1 + c) % n_head for c in range(n_head)]
    depth = heads_here * HD
    loads[0].wait()
    place(qkv[:, QH * HD :], kx_send, kx_recv, kxs_sem, kxr_sem)

    def place_query(c):
        query = qkv[:, pl.ds(pl.multiple_of(partner(c) * depth, HD), depth)]
        place(query, x_send.at[c], x_recv.at[c], xs_sem.at[c], xr_sem.at[c])

    loads[1].wait()
    load_w.start()
    place_query(0)

    across = jnp.broadcast_to(source[...].astype(f32), (tok, tok))
    before = (across.T < across).astype(f32).astype(bf16)
    rlow, rhigh = one_hot_slots(comes, dot(comes.astype(f32).astype(bf16), before), n_seq, cap)
    r_one[0], r_one[1] = rlow.astype(bf16), rhigh.astype(bf16)
    rt_one[0], rt_one[1] = rlow.T.astype(bf16), rhigh.T.astype(bf16)
    kv_rows[...] = gather(kx_recv, kxr_sem)

    def kv_of(block):
        kv = (block * heads_here) // shared
        key = kv_rows[:, pl.ds(pl.multiple_of(kv * HD, HD), HD)]
        value = kv_rows[:, pl.ds(pl.multiple_of((KVH + kv) * HD, HD), HD)]
        return jnp.concatenate([key, value], axis=1)

    kv_recv[pl.ds(head, 1)] = kv_of(head)[None]
    for c in range(1, n_head):
        to = (head + c) % n_head
        k_send[c] = kv_of(to)
        pltpu.make_async_remote_copy(
            src_ref=k_send.at[c], dst_ref=kv_recv.at[head],
            send_sem=ks_sem.at[c], recv_sem=kr_sem.at[head],
            device_id=(seq, to), device_id_type=MESH,
        ).start()

    for c in range(n_head):
        if c + 1 < n_head:
            place_query(c + 1)
        if c == n_head - 1 and n_head == 4:
            continue
        rows = gather(x_recv.at[c], xr_sem.at[c])
        to = partner(c)
        z_send[c] = rows

        @pl.when(to == head)
        def _():
            q_recv[pl.ds(head, 1)] = z_send[pl.ds(c, 1)]

        @pl.when(to != head)
        def _():
            pltpu.make_async_remote_copy(
                src_ref=z_send.at[c], dst_ref=q_recv.at[head],
                send_sem=zs_sem.at[c], recv_sem=zr_sem.at[head],
                device_id=(seq, to), device_id_type=MESH,
            ).start()

    @pl.loop(1, n_head)
    def _(i):
        other = (head + i) % n_head
        wait_bytes(kv_recv.at[other], kr_sem.at[other])

    load_w.wait()
    factor = HD ** (-0.5) * float(np.log2(np.e))

    def attend(i):
        span = (i + 1) * tok
        keys = kv_recv[: i + 1, :, :HD].reshape(span, HD)
        values = kv_recv[: i + 1, :, HD:].reshape(span, HD)
        first = jnp.broadcast_to(starts[:, i * tok : (i + 1) * tok].astype(f32), (tok, tok)).T[:, :1]
        kplace = lax.broadcasted_iota(jnp.int32, (tok, span), 1)
        qplace = lax.broadcasted_iota(jnp.int32, (tok, span), 0) + i * tok
        visible = (kplace <= qplace) & (kplace >= first.astype(jnp.int32))
        for a in range(heads_here):
            scores = lax.dot_general(
                q_recv[i, :, a * HD : (a + 1) * HD], keys, (((1,), (1,)), ((), ())), preferred_element_type=f32
            )
            scores = jnp.where(visible, scores, -1e30)
            top = jnp.max(scores, axis=-1, keepdims=True)
            weights = jnp.exp2((scores - top) * factor)
            total = jnp.sum(weights, axis=-1, keepdims=True)
            attn[i, :, a * HD : (a + 1) * HD] = (dot(weights.astype(bf16), values) / total).astype(bf16)

    def partial(block, j):
        return dot(attn[block], w_vmem[:, pl.ds(pl.multiple_of(j * cols, cols), cols)])

    def step(block, j):
        up = block > head
        slot = jnp.where(up, block + 1, block)
        acc[...] = partial(block, j)

        @pl.when((head > 0) & (head < n_head - 1))
        def _():
            wait_bytes(s_recv.at[slot, j], sr_sem.at[slot, j])
            acc[...] += s_recv[slot, j].astype(f32)

        s_send[block, j] = acc[...].astype(bf16)
        pltpu.make_async_remote_copy(
            src_ref=s_send.at[block, j], dst_ref=s_recv.at[slot, j],
            send_sem=ss_sem.at[block, j], recv_sem=sr_sem.at[slot, j],
            device_id=(seq, jnp.where(up, head + 1, head - 1)), device_id_type=MESH,
        ).start()

    end = (head == 0) | (head == n_head - 1)

    def chain(block):
        @pl.loop(0, jobs)
        def _(j):
            step(block, j)

    quarter = cols // 2

    def own(j):
        acc[...] = partial(head, j)

        @pl.when(head > 0)
        def _():
            wait_bytes(s_recv.at[head + 1, j], sr_sem.at[head + 1, j])
            acc[...] += s_recv[head + 1, j].astype(f32)

        @pl.when(head < n_head - 1)
        def _():
            wait_bytes(s_recv.at[head, j], sr_sem.at[head, j])
            acc[...] += s_recv[head, j].astype(f32)

        proj = acc[...].astype(bf16)
        back = (dot(r_one[0], proj[:, :quarter]) + dot(r_one[1], proj[:, quarter:])).astype(bf16)
        b_send[j] = back.reshape(n_seq, 2 * cap, quarter)
        b_recv[j, pl.ds(seq, 1)] = b_send[j, pl.ds(seq, 1)]

        @pl.loop(1, n_seq)
        def _(i):
            peer = (seq + i) % n_seq
            pltpu.make_async_remote_copy(
                src_ref=b_send.at[j, peer], dst_ref=b_recv.at[j, seq],
                send_sem=bs_sem.at[j], recv_sem=br_sem.at[j],
                device_id=(peer, head), device_id_type=MESH,
            ).start()

    def paced(c, j):
        older = partner(c) if c == 0 else jnp.where(j >= 2, partner(c), partner(c - 1))
        at = (j + jobs - 2) % jobs
        wait_bytes(s_send.at[older, at], ss_sem.at[older, at])
        step(partner(c), j)

    order = [0, n_head - 1] + list(range(1, n_head - 1))

    @pl.loop(0, n_head)
    def _(t):
        block = partner(order[0])
        for place_in, c in enumerate(order):
            block = jnp.where(t == place_in, partner(c), block)

        @pl.when(t == 1)
        def _():
            for side in range(2):
                pt_one[side] = p_one[side].astype(f32).T.astype(bf16)
            if n_head == 4:
                q_recv[pl.ds(head, 1)] = gather(x_recv.at[n_head - 1], xr_sem.at[n_head - 1])[None]

        @pl.when(block != head)
        def _():
            wait_bytes(q_recv.at[block], zr_sem.at[block])

        for i in range(n_head):
            pl.when(block == i)(functools.partial(attend, i))

        if n_head != 4:

            @pl.when((block != head) & end)
            def _():
                chain(block)
        else:

            @pl.when(end & (t == 0))
            def _():
                @pl.loop(0, 2)
                def _(j):
                    step(partner(0), j)

            @pl.when(end & (t == 1))
            def _():
                @pl.loop(2, jobs)
                def _(j):
                    paced(0, j)

            @pl.when(end & (t == 2))
            def _():
                @pl.loop(0, 2)
                def _(j):
                    paced(1, j)

    if n_head == 4:

        @pl.when(end)
        def _():
            @pl.loop(2, jobs)
            def _(j):
                paced(1, j)

            @pl.loop(0, jobs)
            def _(j):
                paced(2, j)
                own(j)

        @pl.when(jnp.logical_not(end))
        def _():
            @pl.loop(0, jobs)
            def _(j):
                step(partner(2), j)
                step(partner(0), j)

            chain(partner(1))

            @pl.loop(0, jobs)
            def _(j):
                own(j)

    else:

        @pl.when(jnp.logical_not(end))
        def _():
            @pl.loop(0, n_head - 1)
            def _(t):
                above, below = n_head - 1 - t, t

                @pl.loop(0, jobs)
                def _(j):
                    @pl.when(above > head)
                    def _():
                        step(above, j)

                    @pl.when(below < head)
                    def _():
                        step(below, j)

        @pl.loop(0, jobs)
        def _(j):
            own(j)

    for j in range(jobs):
        wait_bytes(b_recv.at[j, pl.ds(0, n_seq - 1)], br_sem.at[j])
        arrived = b_recv[j].reshape(slots, quarter)
        mine = jnp.concatenate([dot(pt_one[0], arrived), dot(pt_one[1], arrived)], axis=1)
        out[:, j * cols : (j + 1) * cols] = mine.astype(bf16)

    wait_bytes(kx_send.at[pl.ds(0, n_seq - 1)], kxs_sem)
    for c in range(n_head):
        wait_bytes(x_send.at[c, pl.ds(0, n_seq - 1)], xs_sem.at[c])
        if c > 0:
            wait_bytes(k_send.at[c], ks_sem.at[c])

        @pl.when(partner(c) != head)
        def _():
            wait_bytes(z_send.at[c], zs_sem.at[c])

    @pl.loop(0, jobs)
    def _(j):
        wait_bytes(b_send.at[j, pl.ds(0, n_seq - 1)], bs_sem.at[j])

        @pl.loop(1, n_head)
        def _(i):
            block = (head + i) % n_head
            left = (block == partner(n_head - 2)) & (j >= jobs - 2) if n_head == 4 else block != head

            @pl.when(jnp.logical_not(end) | left)
            def _():
                wait_bytes(s_send.at[block, j], ss_sem.at[block, j])


def finish(mine, residual, gain, out_res, out_norm):
    f32, bf16 = jnp.float32, jnp.bfloat16
    stream = (residual[...].astype(f32) + mine[...].astype(f32)).astype(bf16)
    out_res[...] = stream
    wide = stream.astype(f32)
    scale = lax.rsqrt(jnp.mean(wide * wide, axis=-1, keepdims=True) + 1e-06)
    out_norm[...] = (wide * scale * gain[...]).astype(bf16)


def local(qkv, residual, dest_row, source_row, doc_start, out_weight, norm_gain):
    n_seq = lax.axis_size("seq")
    n_head = lax.axis_size("head")
    tok, _ = qkv.shape
    depth, model = out_weight.shape
    cap = -(-max(2, 3 * tok // (2 * n_seq)) // 8) * 8
    jobs = 4
    cols = model // jobs
    bf16 = jnp.bfloat16
    dma = pltpu.SemaphoreType.DMA
    vmem = pl.BlockSpec(memory_space=pltpu.VMEM)
    hbm = pl.BlockSpec(memory_space=pltpu.HBM)
    scratch = [
        pltpu.VMEM(qkv.shape, bf16),
        pltpu.VMEM((depth, model), bf16),
        pltpu.VMEM((2, n_seq * 2 * cap, tok), bf16),
        pltpu.VMEM((2, tok, n_seq * 2 * cap), bf16),
        pltpu.VMEM((2, n_seq * 2 * cap, tok), bf16),
        pltpu.VMEM((2, tok, n_seq * 2 * cap), bf16),
        pltpu.VMEM((n_seq, 2 * cap, KVH * HD), bf16),
        pltpu.VMEM((n_seq, 2 * cap, KVH * HD), bf16),
        pltpu.VMEM((n_head, n_seq, 2 * cap, depth // 2), bf16),
        pltpu.VMEM((n_head, n_seq, 2 * cap, depth // 2), bf16),
        pltpu.VMEM((tok, 2 * KVH * HD), bf16),
        pltpu.VMEM((n_head, tok, 2 * HD), bf16),
        pltpu.VMEM((n_head, tok, 2 * HD), bf16),
        pltpu.VMEM((n_head, tok, depth), bf16),
        pltpu.VMEM((n_head, tok, depth), bf16),
        pltpu.VMEM((n_head, tok, depth), bf16),
        pltpu.VMEM((n_head, jobs, tok, cols), bf16),
        pltpu.VMEM((n_head + 1, jobs, tok, cols), bf16),
        pltpu.VMEM((tok, cols), jnp.float32),
        pltpu.VMEM((jobs, n_seq, 2 * cap, cols // 2), bf16),
        pltpu.VMEM((jobs, n_seq, 2 * cap, cols // 2), bf16),
        dma((2,)),
        dma,
        dma,
        dma,
        dma((n_head,)),
        dma((n_head,)),
        dma((n_head,)),
        dma((n_head,)),
        dma((n_head,)),
        dma((n_head,)),
        dma((n_head, jobs)),
        dma((n_head + 1, jobs)),
        dma((jobs,)),
        dma((jobs,)),
    ]
    mine = pl.pallas_call(
        functools.partial(kernel, n_seq, n_head, cap, jobs),
        out_shape=jax.ShapeDtypeStruct(residual.shape, bf16),
        in_specs=[hbm, vmem, vmem, vmem, hbm],
        out_specs=vmem,
        scratch_shapes=scratch,
        compiler_params=pltpu.CompilerParams(
            collective_id=0, has_side_effects=True, vmem_limit_bytes=54 * 1024 * 1024
        ),
        name="layer",
    )(
        qkv,
        dest_row.reshape(1, tok),
        source_row.reshape(1, tok),
        doc_start.reshape(1, tok * n_head),
        out_weight,
    )
    return pl.pallas_call(
        finish,
        out_shape=(jax.ShapeDtypeStruct(residual.shape, bf16), jax.ShapeDtypeStruct(residual.shape, bf16)),
        compiler_params=pltpu.CompilerParams(vmem_limit_bytes=16 * 1024 * 1024),
        name="finish",
    )(mine, residual, norm_gain.reshape(1, model))


def solution(mesh):
    return jax.shard_map(
        local,
        mesh=mesh,
        in_specs=(
            P(("seq", "head"), None),
            P(("seq", "head"), None),
            P(("seq", "head")),
            P(("seq", "head")),
            P("seq"),
            P("head", None),
            P(),
        ),
        out_specs=(P(("seq", "head"), None), P(("seq", "head"), None)),
        check_vma=False,
    )
```

```python
import functools

import jax
import jax.numpy as jnp
import numpy as np
from jax import lax
from jax.experimental import pallas as pl
from jax.experimental.pallas import tpu as pltpu
from jax.sharding import PartitionSpec as P

QH = 24
KVH = 4
HD = 128
MESH = pl.DeviceIdType.MESH


def one_hot_slots(member, ranks, n_seq, cap):
    rows = member.shape[1]
    rank = jnp.where(member, ranks.astype(jnp.int32), -4 * cap)
    place = lax.broadcasted_iota(jnp.int32, (n_seq, 2 * cap, rows), 1)
    low = (rank[:, None, :] == place).astype(jnp.float32).reshape(n_seq * 2 * cap, rows)
    high = (rank[:, None, :] + cap == place).astype(jnp.float32).reshape(n_seq * 2 * cap, rows)
    return low, high


def kernel(
    n_seq, n_head, cap, jobs,
    qkv_hbm, dest, source, starts, weight,
    out,
    qkv, w_vmem, p_one, pt_one, r_one, rt_one, kx_send, kx_recv, x_send, x_recv, kv_rows, k_send, kv_recv,
    z_send, q_recv, attn, s_send, s_recv, acc, b_send, b_recv,
    in_sem, w_sem, kxs_sem, kxr_sem, xs_sem, xr_sem, ks_sem, kr_sem, zs_sem, zr_sem, ss_sem, sr_sem, bs_sem, br_sem,
):
    f32, bf16 = jnp.float32, jnp.bfloat16
    seq, head = lax.axis_index("seq"), lax.axis_index("head")
    tok = qkv.shape[0]
    group = tok * n_head
    heads_here = weight.shape[0] // HD
    shared = QH // KVH
    cols = weight.shape[1] // jobs
    slots = n_seq * 2 * cap

    def dot(a, b):
        return jnp.dot(a, b, preferred_element_type=f32)

    def wait_bytes(ref, sem):
        pltpu.make_async_copy(ref, ref, sem).wait()

    loads = [
        pltpu.make_async_copy(qkv_hbm.at[:, part], qkv.at[:, part], in_sem.at[at])
        for at, part in enumerate((slice(QH * HD, None), slice(0, QH * HD)))
    ]
    for load in loads:
        load.start()
    load_w = pltpu.make_async_copy(weight, w_vmem, w_sem)

    barrier = pltpu.get_barrier_semaphore()

    @pl.loop(1, n_seq)
    def _(i):
        pl.semaphore_signal(barrier, inc=1, device_id=((seq + i) % n_seq, head), device_id_type=MESH)

    @pl.loop(1, n_head)
    def _(i):
        pl.semaphore_signal(barrier, inc=1, device_id=(seq, (head + i) % n_head), device_id_type=MESH)

    bounds = lax.broadcasted_iota(jnp.int32, (n_seq, tok), 0) * group
    goes = (dest[...] >= bounds) & (dest[...] < bounds + group)
    comes = (source[...] >= bounds) & (source[...] < bounds + group)
    earlier = lax.broadcasted_iota(jnp.int32, (tok, tok), 0) < lax.broadcasted_iota(jnp.int32, (tok, tok), 1)
    low, high = one_hot_slots(goes, dot(goes.astype(f32).astype(bf16), earlier.astype(f32).astype(bf16)), n_seq, cap)
    p_one[0], p_one[1] = low.astype(bf16), high.astype(bf16)

    pl.semaphore_wait(barrier, n_seq + n_head - 2)

    def partner(c):
        if n_head == 4:
            mirror = n_head - 1 - head
            return [mirror, (head + 2) % n_head, (mirror + 2) % n_head, head][c]
        return (shifts[c] - head + n_head) % n_head

    def place(x, send, recv, s_sem, r_sem):
        side = x.shape[1] // 2
        placed = (dot(p_one[0], x[:, :side]) + dot(p_one[1], x[:, side:])).astype(bf16)
        send[...] = placed.reshape(n_seq, 2 * cap, side)
        recv[pl.ds(seq, 1)] = send[pl.ds(seq, 1)]

        @pl.loop(1, n_seq)
        def _(i):
            peer = (seq + i) % n_seq
            pltpu.make_async_remote_copy(
                src_ref=send.at[peer], dst_ref=recv.at[seq],
                send_sem=s_sem, recv_sem=r_sem,
                device_id=(peer, head), device_id_type=MESH,
            ).start()

    def gather(recv, r_sem):
        wait_bytes(recv.at[pl.ds(0, n_seq - 1)], r_sem)
        arrived = recv[...].reshape(slots, recv.shape[2])
        return jnp.concatenate([dot(rt_one[0], arrived), dot(rt_one[1], arrived)], axis=1).astype(bf16)

    shifts = [(n_head - 1 + c) % n_head for c in range(n_head)]
    depth = heads_here * HD
    loads[0].wait()
    place(qkv[:, QH * HD :], kx_send, kx_recv, kxs_sem, kxr_sem)

    def place_query(c):
        query = qkv[:, pl.ds(pl.multiple_of(partner(c) * depth, HD), depth)]
        place(query, x_send.at[c], x_recv.at[c], xs_sem.at[c], xr_sem.at[c])

    loads[1].wait()
    load_w.start()
    place_query(0)

    across = jnp.broadcast_to(source[...].astype(f32), (tok, tok))
    before = (across.T < across).astype(f32).astype(bf16)
    rlow, rhigh = one_hot_slots(comes, dot(comes.astype(f32).astype(bf16), before), n_seq, cap)
    r_one[0], r_one[1] = rlow.astype(bf16), rhigh.astype(bf16)
    rt_one[0], rt_one[1] = rlow.T.astype(bf16), rhigh.T.astype(bf16)
    kv_rows[...] = gather(kx_recv, kxr_sem)

    def kv_of(block):
        kv = (block * heads_here) // shared
        key = kv_rows[:, pl.ds(pl.multiple_of(kv * HD, HD), HD)]
        value = kv_rows[:, pl.ds(pl.multiple_of((KVH + kv) * HD, HD), HD)]
        return jnp.concatenate([key, value], axis=1)

    kv_recv[pl.ds(head, 1)] = kv_of(head)[None]
    for c in range(1, n_head):
        to = (head + c) % n_head
        k_send[c] = kv_of(to)
        pltpu.make_async_remote_copy(
            src_ref=k_send.at[c], dst_ref=kv_recv.at[head],
            send_sem=ks_sem.at[c], recv_sem=kr_sem.at[head],
            device_id=(seq, to), device_id_type=MESH,
        ).start()

    for c in range(n_head):
        if c + 1 < n_head:
            place_query(c + 1)
        if c == n_head - 1 and n_head == 4:
            continue
        rows = gather(x_recv.at[c], xr_sem.at[c])
        to = partner(c)
        z_send[c] = rows

        @pl.when(to == head)
        def _():
            q_recv[pl.ds(head, 1)] = z_send[pl.ds(c, 1)]

        @pl.when(to != head)
        def _():
            pltpu.make_async_remote_copy(
                src_ref=z_send.at[c], dst_ref=q_recv.at[head],
                send_sem=zs_sem.at[c], recv_sem=zr_sem.at[head],
                device_id=(seq, to), device_id_type=MESH,
            ).start()

    @pl.loop(1, n_head)
    def _(i):
        other = (head + i) % n_head
        wait_bytes(kv_recv.at[other], kr_sem.at[other])

    load_w.wait()
    factor = HD ** (-0.5) * float(np.log2(np.e))

    def attend(i):
        span = (i + 1) * tok
        keys = kv_recv[: i + 1, :, :HD].reshape(span, HD)
        values = kv_recv[: i + 1, :, HD:].reshape(span, HD)
        first = jnp.broadcast_to(starts[:, i * tok : (i + 1) * tok].astype(f32), (tok, tok)).T[:, :1]
        kplace = lax.broadcasted_iota(jnp.int32, (tok, span), 1)
        qplace = lax.broadcasted_iota(jnp.int32, (tok, span), 0) + i * tok
        visible = (kplace <= qplace) & (kplace >= first.astype(jnp.int32))
        for a in range(heads_here):
            scores = lax.dot_general(
                q_recv[i, :, a * HD : (a + 1) * HD], keys, (((1,), (1,)), ((), ())), preferred_element_type=f32
            )
            scores = jnp.where(visible, scores, -1e30)
            top = jnp.max(scores, axis=-1, keepdims=True)
            weights = jnp.exp2((scores - top) * factor)
            total = jnp.sum(weights, axis=-1, keepdims=True)
            attn[i, :, a * HD : (a + 1) * HD] = (dot(weights.astype(bf16), values) / total).astype(bf16)

    def partial(block, j):
        return dot(attn[block], w_vmem[:, pl.ds(pl.multiple_of(j * cols, cols), cols)])

    def step(block, j):
        up = block > head
        slot = jnp.where(up, block + 1, block)
        acc[...] = partial(block, j)

        @pl.when((head > 0) & (head < n_head - 1))
        def _():
            wait_bytes(s_recv.at[slot, j], sr_sem.at[slot, j])
            acc[...] += s_recv[slot, j].astype(f32)

        s_send[block, j] = acc[...].astype(bf16)
        pltpu.make_async_remote_copy(
            src_ref=s_send.at[block, j], dst_ref=s_recv.at[slot, j],
            send_sem=ss_sem.at[block, j], recv_sem=sr_sem.at[slot, j],
            device_id=(seq, jnp.where(up, head + 1, head - 1)), device_id_type=MESH,
        ).start()

    end = (head == 0) | (head == n_head - 1)

    def chain(block):
        @pl.loop(0, jobs)
        def _(j):
            step(block, j)

    quarter = cols // 2

    def own(j):
        acc[...] = partial(head, j)

        @pl.when(head > 0)
        def _():
            wait_bytes(s_recv.at[head + 1, j], sr_sem.at[head + 1, j])
            acc[...] += s_recv[head + 1, j].astype(f32)

        @pl.when(head < n_head - 1)
        def _():
            wait_bytes(s_recv.at[head, j], sr_sem.at[head, j])
            acc[...] += s_recv[head, j].astype(f32)

        proj = acc[...].astype(bf16)
        back = (dot(r_one[0], proj[:, :quarter]) + dot(r_one[1], proj[:, quarter:])).astype(bf16)
        b_send[j] = back.reshape(n_seq, 2 * cap, quarter)
        b_recv[j, pl.ds(seq, 1)] = b_send[j, pl.ds(seq, 1)]

        @pl.loop(1, n_seq)
        def _(i):
            peer = (seq + i) % n_seq
            pltpu.make_async_remote_copy(
                src_ref=b_send.at[j, peer], dst_ref=b_recv.at[j, seq],
                send_sem=bs_sem.at[j], recv_sem=br_sem.at[j],
                device_id=(peer, head), device_id_type=MESH,
            ).start()

    def paced(c, j):
        older = partner(c) if c == 0 else jnp.where(j >= 2, partner(c), partner(c - 1))
        at = (j + jobs - 2) % jobs
        wait_bytes(s_send.at[older, at], ss_sem.at[older, at])
        step(partner(c), j)

    order = [0, n_head - 1] + list(range(1, n_head - 1))

    @pl.loop(0, n_head)
    def _(t):
        block = partner(order[0])
        for place_in, c in enumerate(order):
            block = jnp.where(t == place_in, partner(c), block)

        @pl.when(t == 1)
        def _():
            for side in range(2):
                pt_one[side] = p_one[side].astype(f32).T.astype(bf16)
            if n_head == 4:
                q_recv[pl.ds(head, 1)] = gather(x_recv.at[n_head - 1], xr_sem.at[n_head - 1])[None]

        @pl.when(block != head)
        def _():
            wait_bytes(q_recv.at[block], zr_sem.at[block])

        for i in range(n_head):
            pl.when(block == i)(functools.partial(attend, i))

        if n_head != 4:

            @pl.when((block != head) & end)
            def _():
                chain(block)
        else:

            @pl.when(end & (t == 0))
            def _():
                @pl.loop(0, 2)
                def _(j):
                    step(partner(0), j)

            @pl.when(end & (t == 1))
            def _():
                @pl.loop(2, jobs)
                def _(j):
                    paced(0, j)

            @pl.when(end & (t == 2))
            def _():
                @pl.loop(0, 2)
                def _(j):
                    paced(1, j)

    if n_head == 4:

        @pl.when(end)
        def _():
            @pl.loop(2, jobs)
            def _(j):
                paced(1, j)

            @pl.loop(0, jobs)
            def _(j):
                paced(2, j)
                own(j)

        @pl.when(jnp.logical_not(end))
        def _():
            @pl.loop(0, jobs)
            def _(j):
                step(partner(1), j)
                step(partner(2), j)

            chain(partner(0))

            @pl.loop(0, jobs)
            def _(j):
                own(j)

    else:

        @pl.when(jnp.logical_not(end))
        def _():
            @pl.loop(0, n_head - 1)
            def _(t):
                above, below = n_head - 1 - t, t

                @pl.loop(0, jobs)
                def _(j):
                    @pl.when(above > head)
                    def _():
                        step(above, j)

                    @pl.when(below < head)
                    def _():
                        step(below, j)

        @pl.loop(0, jobs)
        def _(j):
            own(j)

    for j in range(jobs):
        wait_bytes(b_recv.at[j, pl.ds(0, n_seq - 1)], br_sem.at[j])
        arrived = b_recv[j].reshape(slots, quarter)
        mine = jnp.concatenate([dot(pt_one[0], arrived), dot(pt_one[1], arrived)], axis=1)
        out[:, j * cols : (j + 1) * cols] = mine.astype(bf16)

    wait_bytes(kx_send.at[pl.ds(0, n_seq - 1)], kxs_sem)
    for c in range(n_head):
        wait_bytes(x_send.at[c, pl.ds(0, n_seq - 1)], xs_sem.at[c])
        if c > 0:
            wait_bytes(k_send.at[c], ks_sem.at[c])

        @pl.when(partner(c) != head)
        def _():
            wait_bytes(z_send.at[c], zs_sem.at[c])

    @pl.loop(0, jobs)
    def _(j):
        wait_bytes(b_send.at[j, pl.ds(0, n_seq - 1)], bs_sem.at[j])

        @pl.loop(1, n_head)
        def _(i):
            block = (head + i) % n_head
            left = (block == partner(n_head - 2)) & (j >= jobs - 2) if n_head == 4 else block != head

            @pl.when(jnp.logical_not(end) | left)
            def _():
                wait_bytes(s_send.at[block, j], ss_sem.at[block, j])


def finish(mine, residual, gain, out_res, out_norm):
    f32, bf16 = jnp.float32, jnp.bfloat16
    stream = (residual[...].astype(f32) + mine[...].astype(f32)).astype(bf16)
    out_res[...] = stream
    wide = stream.astype(f32)
    scale = lax.rsqrt(jnp.mean(wide * wide, axis=-1, keepdims=True) + 1e-06)
    out_norm[...] = (wide * scale * gain[...]).astype(bf16)


def local(qkv, residual, dest_row, source_row, doc_start, out_weight, norm_gain):
    n_seq = lax.axis_size("seq")
    n_head = lax.axis_size("head")
    tok, _ = qkv.shape
    depth, model = out_weight.shape
    cap = -(-max(2, 3 * tok // (2 * n_seq)) // 8) * 8
    jobs = 4
    cols = model // jobs
    bf16 = jnp.bfloat16
    dma = pltpu.SemaphoreType.DMA
    vmem = pl.BlockSpec(memory_space=pltpu.VMEM)
    hbm = pl.BlockSpec(memory_space=pltpu.HBM)
    scratch = [
        pltpu.VMEM(qkv.shape, bf16),
        pltpu.VMEM((depth, model), bf16),
        pltpu.VMEM((2, n_seq * 2 * cap, tok), bf16),
        pltpu.VMEM((2, tok, n_seq * 2 * cap), bf16),
        pltpu.VMEM((2, n_seq * 2 * cap, tok), bf16),
        pltpu.VMEM((2, tok, n_seq * 2 * cap), bf16),
        pltpu.VMEM((n_seq, 2 * cap, KVH * HD), bf16),
        pltpu.VMEM((n_seq, 2 * cap, KVH * HD), bf16),
        pltpu.VMEM((n_head, n_seq, 2 * cap, depth // 2), bf16),
        pltpu.VMEM((n_head, n_seq, 2 * cap, depth // 2), bf16),
        pltpu.VMEM((tok, 2 * KVH * HD), bf16),
        pltpu.VMEM((n_head, tok, 2 * HD), bf16),
        pltpu.VMEM((n_head, tok, 2 * HD), bf16),
        pltpu.VMEM((n_head, tok, depth), bf16),
        pltpu.VMEM((n_head, tok, depth), bf16),
        pltpu.VMEM((n_head, tok, depth), bf16),
        pltpu.VMEM((n_head, jobs, tok, cols), bf16),
        pltpu.VMEM((n_head + 1, jobs, tok, cols), bf16),
        pltpu.VMEM((tok, cols), jnp.float32),
        pltpu.VMEM((jobs, n_seq, 2 * cap, cols // 2), bf16),
        pltpu.VMEM((jobs, n_seq, 2 * cap, cols // 2), bf16),
        dma((2,)),
        dma,
        dma,
        dma,
        dma((n_head,)),
        dma((n_head,)),
        dma((n_head,)),
        dma((n_head,)),
        dma((n_head,)),
        dma((n_head,)),
        dma((n_head, jobs)),
        dma((n_head + 1, jobs)),
        dma((jobs,)),
        dma((jobs,)),
    ]
    mine = pl.pallas_call(
        functools.partial(kernel, n_seq, n_head, cap, jobs),
        out_shape=jax.ShapeDtypeStruct(residual.shape, bf16),
        in_specs=[hbm, vmem, vmem, vmem, hbm],
        out_specs=vmem,
        scratch_shapes=scratch,
        compiler_params=pltpu.CompilerParams(
            collective_id=0, has_side_effects=True, vmem_limit_bytes=56 * 1024 * 1024
        ),
        name="layer",
    )(
        qkv,
        dest_row.reshape(1, tok),
        source_row.reshape(1, tok),
        doc_start.reshape(1, tok * n_head),
        out_weight,
    )
    return pl.pallas_call(
        finish,
        out_shape=(jax.ShapeDtypeStruct(residual.shape, bf16), jax.ShapeDtypeStruct(residual.shape, bf16)),
        compiler_params=pltpu.CompilerParams(vmem_limit_bytes=16 * 1024 * 1024),
        name="finish",
    )(mine, residual, norm_gain.reshape(1, model))


def solution(mesh):
    return jax.shard_map(
        local,
        mesh=mesh,
        in_specs=(
            P(("seq", "head"), None),
            P(("seq", "head"), None),
            P(("seq", "head")),
            P(("seq", "head")),
            P("seq"),
            P("head", None),
            P(),
        ),
        out_specs=(P(("seq", "head"), None), P(("seq", "head"), None)),
        check_vma=False,
    )
```

```python
import functools

import jax
import jax.numpy as jnp
import numpy as np
from jax import lax
from jax.experimental import pallas as pl
from jax.experimental.pallas import tpu as pltpu
from jax.sharding import PartitionSpec as P

QH = 24
KVH = 4
HD = 128
MESH = pl.DeviceIdType.MESH


def one_hot_slots(member, ranks, n_seq, cap):
    rows = member.shape[1]
    rank = jnp.where(member, ranks.astype(jnp.int32), -4 * cap)
    place = lax.broadcasted_iota(jnp.int32, (n_seq, 2 * cap, rows), 1)
    low = (rank[:, None, :] == place).astype(jnp.float32).reshape(n_seq * 2 * cap, rows)
    high = (rank[:, None, :] + cap == place).astype(jnp.float32).reshape(n_seq * 2 * cap, rows)
    return low, high


def kernel(
    n_seq, n_head, cap, jobs,
    qkv_hbm, dest, source, starts, weight,
    out,
    qkv, w_vmem, p_one, pt_one, r_one, rt_one, kx_send, kx_recv, x_send, x_recv, kv_rows, k_send, kv_recv,
    z_send, q_recv, attn, s_send, s_recv, acc, b_send, b_recv,
    in_sem, w_sem, kxs_sem, kxr_sem, xs_sem, xr_sem, ks_sem, kr_sem, zs_sem, zr_sem, ss_sem, sr_sem, bs_sem, br_sem,
):
    f32, bf16 = jnp.float32, jnp.bfloat16
    seq, head = lax.axis_index("seq"), lax.axis_index("head")
    tok = qkv.shape[0]
    group = tok * n_head
    heads_here = weight.shape[0] // HD
    shared = QH // KVH
    cols = weight.shape[1] // jobs
    slots = n_seq * 2 * cap

    def dot(a, b):
        return jnp.dot(a, b, preferred_element_type=f32)

    def wait_bytes(ref, sem):
        pltpu.make_async_copy(ref, ref, sem).wait()

    loads = [
        pltpu.make_async_copy(qkv_hbm.at[:, part], qkv.at[:, part], in_sem.at[at])
        for at, part in enumerate((slice(QH * HD, None), slice(0, QH * HD)))
    ]
    for load in loads:
        load.start()
    load_w = pltpu.make_async_copy(weight, w_vmem, w_sem)

    barrier = pltpu.get_barrier_semaphore()

    @pl.loop(1, n_seq)
    def _(i):
        pl.semaphore_signal(barrier, inc=1, device_id=((seq + i) % n_seq, head), device_id_type=MESH)

    @pl.loop(1, n_head)
    def _(i):
        pl.semaphore_signal(barrier, inc=1, device_id=(seq, (head + i) % n_head), device_id_type=MESH)

    bounds = lax.broadcasted_iota(jnp.int32, (n_seq, tok), 0) * group
    goes = (dest[...] >= bounds) & (dest[...] < bounds + group)
    comes = (source[...] >= bounds) & (source[...] < bounds + group)
    earlier = lax.broadcasted_iota(jnp.int32, (tok, tok), 0) < lax.broadcasted_iota(jnp.int32, (tok, tok), 1)
    low, high = one_hot_slots(goes, dot(goes.astype(f32).astype(bf16), earlier.astype(f32).astype(bf16)), n_seq, cap)
    p_one[0], p_one[1] = low.astype(bf16), high.astype(bf16)

    pl.semaphore_wait(barrier, n_seq + n_head - 2)

    def partner(c):
        if n_head == 4:
            mirror = n_head - 1 - head
            return [mirror, (head + 2) % n_head, (mirror + 2) % n_head, head][c]
        return (shifts[c] - head + n_head) % n_head

    def place(x, send, recv, s_sem, r_sem):
        side = x.shape[1] // 2
        placed = (dot(p_one[0], x[:, :side]) + dot(p_one[1], x[:, side:])).astype(bf16)
        send[...] = placed.reshape(n_seq, 2 * cap, side)
        recv[pl.ds(seq, 1)] = send[pl.ds(seq, 1)]

        @pl.loop(1, n_seq)
        def _(i):
            peer = (seq + i) % n_seq
            pltpu.make_async_remote_copy(
                src_ref=send.at[peer], dst_ref=recv.at[seq],
                send_sem=s_sem, recv_sem=r_sem,
                device_id=(peer, head), device_id_type=MESH,
            ).start()

    def gather(recv, r_sem):
        wait_bytes(recv.at[pl.ds(0, n_seq - 1)], r_sem)
        arrived = recv[...].reshape(slots, recv.shape[2])
        return jnp.concatenate([dot(rt_one[0], arrived), dot(rt_one[1], arrived)], axis=1).astype(bf16)

    shifts = [(n_head - 1 + c) % n_head for c in range(n_head)]
    depth = heads_here * HD
    loads[0].wait()
    place(qkv[:, QH * HD :], kx_send, kx_recv, kxs_sem, kxr_sem)

    low_t, high_t = low.T, high.T
    pt_one[0], pt_one[1] = low_t.astype(bf16), high_t.astype(bf16)
    across = jnp.broadcast_to(source[...].astype(f32), (tok, tok))
    before = (across.T < across).astype(f32).astype(bf16)
    rlow, rhigh = one_hot_slots(comes, dot(comes.astype(f32).astype(bf16), before), n_seq, cap)
    r_one[0], r_one[1] = rlow.astype(bf16), rhigh.astype(bf16)
    rt_one[0], rt_one[1] = rlow.T.astype(bf16), rhigh.T.astype(bf16)

    def place_query(c):
        query = qkv[:, pl.ds(pl.multiple_of(partner(c) * depth, HD), depth)]
        place(query, x_send.at[c], x_recv.at[c], xs_sem.at[c], xr_sem.at[c])

    loads[1].wait()
    load_w.start()
    place_query(0)
    kv_rows[...] = gather(kx_recv, kxr_sem)

    def kv_of(block):
        kv = (block * heads_here) // shared
        key = kv_rows[:, pl.ds(pl.multiple_of(kv * HD, HD), HD)]
        value = kv_rows[:, pl.ds(pl.multiple_of((KVH + kv) * HD, HD), HD)]
        return jnp.concatenate([key, value], axis=1)

    kv_recv[pl.ds(head, 1)] = kv_of(head)[None]
    for c in range(1, n_head):
        to = (head + c) % n_head
        k_send[c] = kv_of(to)
        pltpu.make_async_remote_copy(
            src_ref=k_send.at[c], dst_ref=kv_recv.at[head],
            send_sem=ks_sem.at[c], recv_sem=kr_sem.at[head],
            device_id=(seq, to), device_id_type=MESH,
        ).start()

    for c in range(n_head):
        if c + 1 < n_head:
            place_query(c + 1)
        rows = gather(x_recv.at[c], xr_sem.at[c])
        to = partner(c)
        z_send[c] = rows

        @pl.when(to == head)
        def _():
            q_recv[pl.ds(head, 1)] = z_send[pl.ds(c, 1)]

        @pl.when(to != head)
        def _():
            pltpu.make_async_remote_copy(
                src_ref=z_send.at[c], dst_ref=q_recv.at[head],
                send_sem=zs_sem.at[c], recv_sem=zr_sem.at[head],
                device_id=(seq, to), device_id_type=MESH,
            ).start()

    @pl.loop(1, n_head)
    def _(i):
        other = (head + i) % n_head
        wait_bytes(kv_recv.at[other], kr_sem.at[other])

    load_w.wait()
    factor = HD ** (-0.5) * float(np.log2(np.e))

    def attend(i):
        span = (i + 1) * tok
        keys = kv_recv[: i + 1, :, :HD].reshape(span, HD)
        values = kv_recv[: i + 1, :, HD:].reshape(span, HD)
        first = jnp.broadcast_to(starts[:, i * tok : (i + 1) * tok].astype(f32), (tok, tok)).T[:, :1]
        kplace = lax.broadcasted_iota(jnp.int32, (tok, span), 1)
        qplace = lax.broadcasted_iota(jnp.int32, (tok, span), 0) + i * tok
        visible = (kplace <= qplace) & (kplace >= first.astype(jnp.int32))
        for a in range(heads_here):
            scores = lax.dot_general(
                q_recv[i, :, a * HD : (a + 1) * HD], keys, (((1,), (1,)), ((), ())), preferred_element_type=f32
            )
            scores = jnp.where(visible, scores, -1e30)
            top = jnp.max(scores, axis=-1, keepdims=True)
            weights = jnp.exp2((scores - top) * factor)
            total = jnp.sum(weights, axis=-1, keepdims=True)
            attn[i, :, a * HD : (a + 1) * HD] = (dot(weights.astype(bf16), values) / total).astype(bf16)

    def partial(block, j):
        return dot(attn[block], w_vmem[:, pl.ds(pl.multiple_of(j * cols, cols), cols)])

    def step(block, j):
        up = block > head
        slot = jnp.where(up, block + 1, block)
        acc[...] = partial(block, j)

        @pl.when((head > 0) & (head < n_head - 1))
        def _():
            wait_bytes(s_recv.at[slot, j], sr_sem.at[slot, j])
            acc[...] += s_recv[slot, j].astype(f32)

        s_send[block, j] = acc[...].astype(bf16)
        pltpu.make_async_remote_copy(
            src_ref=s_send.at[block, j], dst_ref=s_recv.at[slot, j],
            send_sem=ss_sem.at[block, j], recv_sem=sr_sem.at[slot, j],
            device_id=(seq, jnp.where(up, head + 1, head - 1)), device_id_type=MESH,
        ).start()

    end = (head == 0) | (head == n_head - 1)

    def chain(block):
        @pl.loop(0, jobs)
        def _(j):
            step(block, j)

    quarter = cols // 2

    def own(j):
        acc[...] = partial(head, j)

        @pl.when(head > 0)
        def _():
            wait_bytes(s_recv.at[head + 1, j], sr_sem.at[head + 1, j])
            acc[...] += s_recv[head + 1, j].astype(f32)

        @pl.when(head < n_head - 1)
        def _():
            wait_bytes(s_recv.at[head, j], sr_sem.at[head, j])
            acc[...] += s_recv[head, j].astype(f32)

        proj = acc[...].astype(bf16)
        back = (dot(r_one[0], proj[:, :quarter]) + dot(r_one[1], proj[:, quarter:])).astype(bf16)
        b_send[j] = back.reshape(n_seq, 2 * cap, quarter)
        b_recv[j, pl.ds(seq, 1)] = b_send[j, pl.ds(seq, 1)]

        @pl.loop(1, n_seq)
        def _(i):
            peer = (seq + i) % n_seq
            pltpu.make_async_remote_copy(
                src_ref=b_send.at[j, peer], dst_ref=b_recv.at[j, seq],
                send_sem=bs_sem.at[j], recv_sem=br_sem.at[j],
                device_id=(peer, head), device_id_type=MESH,
            ).start()

    def paced(c, j):
        older = partner(c) if c == 0 else jnp.where(j >= 2, partner(c), partner(c - 1))
        at = (j + jobs - 2) % jobs
        wait_bytes(s_send.at[older, at], ss_sem.at[older, at])
        step(partner(c), j)

    order = [0, n_head - 1] + list(range(1, n_head - 1))

    @pl.loop(0, n_head)
    def _(t):
        block = partner(order[0])
        for place_in, c in enumerate(order):
            block = jnp.where(t == place_in, partner(c), block)

        @pl.when(block != head)
        def _():
            wait_bytes(q_recv.at[block], zr_sem.at[block])

        for i in range(n_head):
            pl.when(block == i)(functools.partial(attend, i))

        if n_head != 4:

            @pl.when((block != head) & end)
            def _():
                chain(block)
        else:

            @pl.when(end & (t == 0))
            def _():
                @pl.loop(0, 2)
                def _(j):
                    step(partner(0), j)

            @pl.when(end & (t == 1))
            def _():
                @pl.loop(2, jobs)
                def _(j):
                    paced(0, j)

            @pl.when(end & (t == 2))
            def _():
                @pl.loop(0, 2)
                def _(j):
                    paced(1, j)

    if n_head == 4:

        @pl.when(end)
        def _():
            @pl.loop(2, jobs)
            def _(j):
                paced(1, j)

            @pl.loop(0, jobs)
            def _(j):
                paced(2, j)
                own(j)

        @pl.when(jnp.logical_not(end))
        def _():
            @pl.loop(0, jobs)
            def _(j):
                step(partner(1), j)
                step(partner(2), j)

            chain(partner(0))

            @pl.loop(0, jobs)
            def _(j):
                own(j)

    else:

        @pl.when(jnp.logical_not(end))
        def _():
            @pl.loop(0, n_head - 1)
            def _(t):
                above, below = n_head - 1 - t, t

                @pl.loop(0, jobs)
                def _(j):
                    @pl.when(above > head)
                    def _():
                        step(above, j)

                    @pl.when(below < head)
                    def _():
                        step(below, j)

        @pl.loop(0, jobs)
        def _(j):
            own(j)

    for j in range(jobs):
        wait_bytes(b_recv.at[j, pl.ds(0, n_seq - 1)], br_sem.at[j])
        arrived = b_recv[j].reshape(slots, quarter)
        mine = jnp.concatenate([dot(pt_one[0], arrived), dot(pt_one[1], arrived)], axis=1)
        out[:, j * cols : (j + 1) * cols] = mine.astype(bf16)

    wait_bytes(kx_send.at[pl.ds(0, n_seq - 1)], kxs_sem)
    for c in range(n_head):
        wait_bytes(x_send.at[c, pl.ds(0, n_seq - 1)], xs_sem.at[c])
        if c > 0:
            wait_bytes(k_send.at[c], ks_sem.at[c])

        @pl.when(partner(c) != head)
        def _():
            wait_bytes(z_send.at[c], zs_sem.at[c])

    @pl.loop(0, jobs)
    def _(j):
        wait_bytes(b_send.at[j, pl.ds(0, n_seq - 1)], bs_sem.at[j])

        @pl.loop(1, n_head)
        def _(i):
            block = (head + i) % n_head
            left = (block == partner(n_head - 2)) & (j >= jobs - 2) if n_head == 4 else block != head

            @pl.when(jnp.logical_not(end) | left)
            def _():
                wait_bytes(s_send.at[block, j], ss_sem.at[block, j])


def finish(mine, residual, gain, out_res, out_norm):
    f32, bf16 = jnp.float32, jnp.bfloat16
    stream = (residual[...].astype(f32) + mine[...].astype(f32)).astype(bf16)
    out_res[...] = stream
    wide = stream.astype(f32)
    scale = lax.rsqrt(jnp.mean(wide * wide, axis=-1, keepdims=True) + 1e-06)
    out_norm[...] = (wide * scale * gain[...]).astype(bf16)


def local(qkv, residual, dest_row, source_row, doc_start, out_weight, norm_gain):
    n_seq = lax.axis_size("seq")
    n_head = lax.axis_size("head")
    tok, _ = qkv.shape
    depth, model = out_weight.shape
    cap = -(-max(2, 3 * tok // (2 * n_seq)) // 8) * 8
    jobs = 8
    cols = model // jobs
    bf16 = jnp.bfloat16
    dma = pltpu.SemaphoreType.DMA
    vmem = pl.BlockSpec(memory_space=pltpu.VMEM)
    hbm = pl.BlockSpec(memory_space=pltpu.HBM)
    scratch = [
        pltpu.VMEM(qkv.shape, bf16),
        pltpu.VMEM((depth, model), bf16),
        pltpu.VMEM((2, n_seq * 2 * cap, tok), bf16),
        pltpu.VMEM((2, tok, n_seq * 2 * cap), bf16),
        pltpu.VMEM((2, n_seq * 2 * cap, tok), bf16),
        pltpu.VMEM((2, tok, n_seq * 2 * cap), bf16),
        pltpu.VMEM((n_seq, 2 * cap, KVH * HD), bf16),
        pltpu.VMEM((n_seq, 2 * cap, KVH * HD), bf16),
        pltpu.VMEM((n_head, n_seq, 2 * cap, depth // 2), bf16),
        pltpu.VMEM((n_head, n_seq, 2 * cap, depth // 2), bf16),
        pltpu.VMEM((tok, 2 * KVH * HD), bf16),
        pltpu.VMEM((n_head, tok, 2 * HD), bf16),
        pltpu.VMEM((n_head, tok, 2 * HD), bf16),
        pltpu.VMEM((n_head, tok, depth), bf16),
        pltpu.VMEM((n_head, tok, depth), bf16),
        pltpu.VMEM((n_head, tok, depth), bf16),
        pltpu.VMEM((n_head, jobs, tok, cols), bf16),
        pltpu.VMEM((n_head + 1, jobs, tok, cols), bf16),
        pltpu.VMEM((tok, cols), jnp.float32),
        pltpu.VMEM((jobs, n_seq, 2 * cap, cols // 2), bf16),
        pltpu.VMEM((jobs, n_seq, 2 * cap, cols // 2), bf16),
        dma((2,)),
        dma,
        dma,
        dma,
        dma((n_head,)),
        dma((n_head,)),
        dma((n_head,)),
        dma((n_head,)),
        dma((n_head,)),
        dma((n_head,)),
        dma((n_head, jobs)),
        dma((n_head + 1, jobs)),
        dma((jobs,)),
        dma((jobs,)),
    ]
    mine = pl.pallas_call(
        functools.partial(kernel, n_seq, n_head, cap, jobs),
        out_shape=jax.ShapeDtypeStruct(residual.shape, bf16),
        in_specs=[hbm, vmem, vmem, vmem, hbm],
        out_specs=vmem,
        scratch_shapes=scratch,
        compiler_params=pltpu.CompilerParams(
            collective_id=0, has_side_effects=True, vmem_limit_bytes=56 * 1024 * 1024
        ),
        name="layer",
    )(
        qkv,
        dest_row.reshape(1, tok),
        source_row.reshape(1, tok),
        doc_start.reshape(1, tok * n_head),
        out_weight,
    )
    return pl.pallas_call(
        finish,
        out_shape=(jax.ShapeDtypeStruct(residual.shape, bf16), jax.ShapeDtypeStruct(residual.shape, bf16)),
        compiler_params=pltpu.CompilerParams(vmem_limit_bytes=16 * 1024 * 1024),
        name="finish",
    )(mine, residual, norm_gain.reshape(1, model))


def solution(mesh):
    return jax.shard_map(
        local,
        mesh=mesh,
        in_specs=(
            P(("seq", "head"), None),
            P(("seq", "head"), None),
            P(("seq", "head")),
            P(("seq", "head")),
            P("seq"),
            P("head", None),
            P(),
        ),
        out_specs=(P(("seq", "head"), None), P(("seq", "head"), None)),
        check_vma=False,
    )
```
